32 devices in a mesh: fsdp: 16 (over z, y, core), tp: 2 (over x).
Axes of the slice: x: 2, y: 2, z: 4, core: 2. Of those that a mesh axis runs over, the one named last changes fastest.
Arguments:
- tokens: bfloat16 [8192, 1280], P(('fsdp', 'tp')), may hold values from -6 to 6
- seg_starts: int32 [16, 8], P('fsdp'), may hold values from 0 to 511, as said below
- gain_attn: float32 [1280], replicated, may hold values from 0.5 to 1.5
- gain_mlp: float32 [1280], replicated, may hold values from 0.5 to 1.5
- query_scale: float32 [80], replicated, may hold values from -0.5 to 1
- w_query: bfloat16 [1280, 1280], P('fsdp', 'tp'), may hold values from -0.15625 to 0.15625
- w_key: bfloat16 [1280, 1280], P('fsdp', 'tp'), may hold values from -0.15625 to 0.15625
- w_value: bfloat16 [1280, 1280], P('fsdp', 'tp'), may hold values from -0.15625 to 0.15625
- w_out: bfloat16 [1280, 1280], P('tp', 'fsdp'), may hold values from -1.25 to 1.25
- w_up: bfloat16 [1280, 1280], P('fsdp', 'tp'), may hold values from -0.15625 to 0.15625
- w_down: bfloat16 [1280, 1280], P('tp', 'fsdp'), may hold values from -0.15625 to 0.15625
- cotangent: bfloat16 [8192, 1280], P(('fsdp', 'tp')), may hold values from -6 to 6
Outputs:
- result: bfloat16 [8192, 1280], P(('fsdp', 'tp'))
- grad_tokens: float32 [8192, 1280], P(('fsdp', 'tp'))
- grad_gain_attn: float32 [1280], replicated
- grad_gain_mlp: float32 [1280], replicated
- grad_query_scale: float32 [80], replicated
- grad_w_query: float32 [1280, 1280], P('fsdp', 'tp')
- grad_w_key: float32 [1280, 1280], P('fsdp', 'tp')
- grad_w_value: float32 [1280, 1280], P('fsdp', 'tp')
- grad_w_out: float32 [1280, 1280], P('tp', 'fsdp')
- grad_w_up: float32 [1280, 1280], P('fsdp', 'tp')
- grad_w_down: float32 [1280, 1280], P('tp', 'fsdp')
The draws below stay inside these ranges and needn't reach their ends.
Inputs may be any that keep to these rules, and one draw needn't show every extreme that they name: `seg_starts`: in each row the starts rise strictly and the first is 0; a series runs from its start to the next start, the last to the row's end. In the first row the last series has one position.
All inputs are finite; a program needn't handle non-finite values.
Results may differ from the reference program's by a relative error of at most 0.012.
Values may be sent and summed in bfloat16 or wider, within the bound.
No kernel may reach another device: no remote copies, remote signals or barrier semaphores. Data moves between devices by JAX's collectives and lax.ppermute only.
A program may use at most 128 MiB of HBM per device.

```python
import math
import jax
import jax.numpy as jnp
from jax import lax

D = 1280
HEADS = 16
HD = 80
FF = 1280
NSEG = 8
ROW = 512
ROWS = 16
TOKENS = 8192
QBLK = 512
N_TP = 2


def draw_seg_starts(key, part):
    key = jax.random.fold_in(key, 7)
    length_key, pick_key = jax.random.split(key)
    span = max(1, ROW // (N_TP * NSEG))
    lengths = jax.random.randint(length_key, (ROWS, NSEG), 1, span + 1)
    slots = jnp.arange(NSEG, dtype=jnp.int32)[None, :]
    rows = jnp.arange(ROWS, dtype=jnp.int32)[:, None]
    lengths = jnp.where((rows == 0) & (slots == NSEG - 1), 1, lengths)
    longest = jax.random.randint(pick_key, (ROWS, 1), 0, NSEG - 1)
    chosen = slots == longest
    others = jnp.sum(jnp.where(chosen, 0, lengths), axis=1, keepdims=True)
    lengths = jnp.where(chosen, ROW - others, lengths)
    starts = jnp.cumsum(lengths, axis=1) - lengths
    return starts.astype(jnp.int32)


def block_levels(stream_key, extent, cuts, smallest, largest):
    def one(dim, parts):
        steps = jax.random.uniform(jax.random.fold_in(jax.random.fold_in(stream_key, 6), dim), (parts,), jnp.float32, smallest / len(cuts), largest / len(cuts))
        return jnp.repeat(jnp.exp(steps), extent[dim] // parts).reshape((-1,) + (1,) * (len(extent) - dim - 1))

    loudness = one(*cuts[0])
    for cut in cuts[1:]:
        loudness = loudness * one(*cut)
    return loudness


def scatter_about(key, dims, deviation, limit, cuts=(), kind=jnp.bfloat16):
    values = jax.random.normal(key, dims, jnp.float32) * deviation
    if len(cuts) > 0:
        values = block_levels(key, dims, cuts, -0.22, 0.18) * values
    return jnp.clip(values, min=-limit, max=limit).astype(kind)


def setup_inputs(seed: int = 0) -> dict:
    keys = jax.random.split(jax.random.key(seed), 13)
    return {
        "tokens": scatter_about(keys[0], (TOKENS, D), 1.0, 6.0, ((0, 32),)),
        "seg_starts": draw_seg_starts(jax.random.fold_in(keys[12], 71), 0),
        "gain_attn": jnp.clip(1.0 + 0.1 * jax.random.normal(keys[2], (D,), jnp.float32), 0.5, 1.5),
        "gain_mlp": jnp.clip(1.0 + 0.1 * jax.random.normal(keys[3], (D,), jnp.float32), 0.5, 1.5),
        "query_scale": jnp.clip(jax.random.uniform(keys[4], (HD,), jnp.float32, -0.5, 1.0), -0.5, 1.0),
        "w_query": scatter_about(keys[5], (D, D), D ** -0.5, 0.15625, ((0, 16), (1, 2))),
        "w_key": scatter_about(keys[6], (D, D), D ** -0.5, 0.15625, ((0, 16), (1, 2))),
        "w_value": scatter_about(keys[7], (D, D), D ** -0.5, 0.15625, ((0, 16), (1, 2))),
        "w_out": scatter_about(keys[8], (D, D), (D // 64) ** -0.5, 1.25, ((0, 2), (1, 16))),
        "w_up": scatter_about(keys[9], (D, FF), D ** -0.5, 0.15625, ((0, 16), (1, 2))),
        "w_down": scatter_about(keys[10], (FF, D), FF ** -0.5, 0.15625, ((0, 2), (1, 16))),
        "cotangent": scatter_about(keys[11], (TOKENS, D), 1.0, 6.0, ((0, 32),)),
    }


@jax.custom_vjp
def low(v):
    return lax.optimization_barrier(v.astype(jnp.bfloat16)).astype(jnp.float32)

@jax.custom_vjp
def low_back(v):
    return v

def low_keep(v):
    return (low(v), None)

def low_pass(kept, grad):
    return (grad,)

def back_keep(v):
    return (v, None)

def back_low(kept, grad):
    return (low(grad),)
low.defvjp(low_keep, low_pass)
low_back.defvjp(back_keep, back_low)
highest = lax.Precision.HIGHEST
epsilon = 1e-06
softplus_unit = 1.442695041

def inverse_rms(values):
    return lax.rsqrt(lax.optimization_barrier(jnp.mean(values * values, axis=-1, keepdims=True)) + epsilon)

def segment_ids(starts):
    positions = jnp.arange(ROW, dtype=jnp.int32)
    inside = (starts[None, :] <= positions[:, None]).astype(jnp.int32)
    return (positions, lax.optimization_barrier(jnp.sum(inside, axis=1)) - 1)

def attention(query_b, key_b, value_b, positions, series):
    num_blocks = ROW // QBLK

    def one_block(inputs):
        query_blk, block_pos, block_series = inputs
        scores = low_back(jnp.einsum('qhd,khd->hqk', query_blk, key_b, precision=highest))
        allowed = (positions[None, :] <= block_pos[:, None]) & (series[None, :] == block_series[:, None])
        scores = jnp.where(allowed[None], scores, -1e+30)
        row_max = lax.optimization_barrier(jnp.max(scores, axis=-1, keepdims=True))
        exponent = jnp.exp(scores - row_max)
        soft = exponent / lax.optimization_barrier(jnp.sum(exponent, axis=-1, keepdims=True))
        return jnp.einsum('hqk,khd->qhd', low(soft), value_b, precision=highest)
    mixed = lax.map(jax.checkpoint(one_block), (query_b.reshape(num_blocks, QBLK, HEADS, HD), positions.reshape(num_blocks, QBLK), series.reshape(num_blocks, QBLK)))
    return mixed.reshape(ROW, D)

def layer(row_tokens, starts, gain_attn, gain_mlp, query_scale, w_query, w_key, w_value, w_out, w_up, w_down):
    positions, series = segment_ids(starts)
    normed_one = low(row_tokens * inverse_rms(row_tokens) * gain_attn)
    scaling = softplus_unit / math.sqrt(HD) * jax.nn.softplus(query_scale)
    query = low_back(jnp.dot(normed_one, w_query, precision=highest)).reshape(ROW, HEADS, HD)
    query_b = low(query * scaling)
    key_b = low(low_back(jnp.dot(normed_one, w_key, precision=highest))).reshape(ROW, HEADS, HD)
    value_b = low(low_back(jnp.dot(normed_one, w_value, precision=highest))).reshape(ROW, HEADS, HD)
    mixed_b = low(low_back(attention(query_b, key_b, value_b, positions, series)))
    middle = row_tokens + low_back(jnp.dot(mixed_b, w_out, precision=highest))
    normed_two = low(middle * inverse_rms(middle) * gain_mlp)
    hidden_b = low(jax.nn.gelu(low_back(jnp.dot(normed_two, w_up, precision=highest))))
    return middle + low_back(jnp.dot(hidden_b, w_down, precision=highest))

def reference(tokens, seg_starts, gain_attn, gain_mlp, query_scale, w_query, w_key, w_value, w_out, w_up, w_down, cotangent):
    params = tuple((param.astype(jnp.float32) for param in (gain_attn, gain_mlp, query_scale, w_query, w_key, w_value, w_out, w_up, w_down)))
    rows_in = tokens.astype(jnp.float32).reshape(ROWS, ROW, D)
    rows_cot = cotangent.astype(jnp.float32).reshape(ROWS, ROW, D)

    def forward(rows_in, params):

        def one_row(carry, inputs):
            row_tokens, starts = inputs
            return (carry, layer(row_tokens, starts, params[0], params[1], params[2], params[3], params[4], params[5], params[6], params[7], params[8]))
        _, outputs = lax.scan(one_row, jnp.zeros((), jnp.float32), (rows_in, seg_starts))
        return outputs
    outputs, pullback = jax.vjp(forward, rows_in, params)
    grad_rows, grads = pullback(rows_cot)
    return (outputs.reshape(TOKENS, D).astype(jnp.bfloat16), grad_rows.reshape(TOKENS, D), grads[0], grads[1], grads[2], grads[3], grads[4], grads[5], grads[6], grads[7], grads[8])
```

```python
import math

import jax
import jax.numpy as jnp
from jax import lax
from jax.sharding import PartitionSpec as P

HD = 80


epsilon = 1e-06
softplus_unit = 1.442695041


def inverse_rms(values):
    return lax.rsqrt(jnp.mean(values * values, axis=-1, keepdims=True) + epsilon)


def norm_backward(resid, inv_scale, gain, dnormed):
    weighted = dnormed * gain
    cubed = inv_scale * inv_scale * inv_scale
    dresid = inv_scale * weighted - resid * cubed * jnp.mean(
        weighted * resid, axis=-1, keepdims=True
    )
    dgain = jnp.sum(dnormed * resid * inv_scale, axis=0)
    return (dresid, dgain)


def segment_ids(starts, length):
    positions = jnp.arange(length, dtype=jnp.int32)
    inside = (starts[None, :] <= positions[:, None]).astype(jnp.int32)
    return (positions, jnp.sum(inside, axis=1) - 1)


def block_scores(query_blk, block_pos, block_series, key_b, positions, series):
    scores = jnp.einsum("qhd,khd->hqk", query_blk, key_b, preferred_element_type=jnp.float32)
    allowed = (positions[None, :] <= block_pos[:, None]) & (
        series[None, :] == block_series[:, None]
    )
    return jnp.where(allowed[None], scores, -1e30)


def attend_forward(query_b, key_b, value_b, positions, series, block_rows):
    num_blocks = query_b.shape[0] // block_rows
    local_heads = query_b.shape[1]

    def one_block(inputs):
        query_blk, block_pos, block_series = inputs
        scores = block_scores(query_blk, block_pos, block_series, key_b, positions, series)
        row_max = jnp.max(scores, axis=-1, keepdims=True)
        exponent = jnp.exp(scores - row_max)
        total = jnp.sum(exponent, axis=-1, keepdims=True)
        soft_b = (exponent / total).astype(jnp.bfloat16)
        mixed = jnp.einsum("hqk,khd->qhd", soft_b, value_b, preferred_element_type=jnp.float32)
        return (mixed, row_max + jnp.log(total))

    mixed, logsum = lax.map(
        one_block,
        (
            query_b.reshape(num_blocks, block_rows, local_heads, HD),
            positions.reshape(num_blocks, block_rows),
            series.reshape(num_blocks, block_rows),
        ),
    )
    return (mixed.reshape(query_b.shape[0], local_heads * HD), logsum)


def attend_backward(query_b, key_b, value_b, dmixed, logsum, positions, series, block_rows):
    num_blocks = query_b.shape[0] // block_rows
    local_heads = query_b.shape[1]

    def one_block(carry, inputs):
        dkey, dvalue = carry
        query_blk, dmixed_blk, block_pos, block_series, logsum_blk = inputs
        scores = block_scores(query_blk, block_pos, block_series, key_b, positions, series)
        soft = jnp.exp(scores - logsum_blk)
        dsoft = jnp.einsum("qhd,khd->hqk", dmixed_blk, value_b, preferred_element_type=jnp.float32)
        inner = jnp.sum(soft * dsoft, axis=-1, keepdims=True)
        dscores = (soft * (dsoft - inner)).astype(jnp.bfloat16)
        dquery_blk = jnp.einsum("hqk,khd->qhd", dscores, key_b, preferred_element_type=jnp.float32)
        dkey = dkey + jnp.einsum(
            "hqk,qhd->khd", dscores, query_blk, preferred_element_type=jnp.float32
        )
        dvalue = dvalue + jnp.einsum(
            "hqk,qhd->khd",
            soft.astype(jnp.bfloat16),
            dmixed_blk,
            preferred_element_type=jnp.float32,
        )
        return ((dkey, dvalue), dquery_blk)

    zeros = jnp.zeros(key_b.shape, jnp.float32)
    inputs = (
        query_b.reshape(num_blocks, block_rows, local_heads, HD),
        dmixed.reshape(num_blocks, block_rows, local_heads, HD),
        positions.reshape(num_blocks, block_rows),
        series.reshape(num_blocks, block_rows),
        logsum,
    )
    (dkey, dvalue), dquery = lax.scan(one_block, (zeros, zeros), inputs)
    return (dquery.reshape(query_b.shape), dkey, dvalue)


def on_device(
    tokens,
    seg_starts,
    gain_attn,
    gain_mlp,
    query_scale,
    w_query,
    w_key,
    w_value,
    w_out,
    w_up,
    w_down,
    cotangent,
):
    gathered = (
        lax.all_gather(w_query, "fsdp", axis=0, tiled=True),
        lax.all_gather(w_key, "fsdp", axis=0, tiled=True),
        lax.all_gather(w_value, "fsdp", axis=0, tiled=True),
        lax.all_gather(w_out, "fsdp", axis=1, tiled=True),
        lax.all_gather(w_up, "fsdp", axis=0, tiled=True),
        lax.all_gather(w_down, "fsdp", axis=1, tiled=True),
    )
    full_query, full_key, full_value, full_out, full_up, full_down = gathered
    local_rows = tokens.shape[0]
    row_length = local_rows * lax.axis_size("tp")
    block_rows = min(512, row_length)
    local_heads = full_query.shape[1] // HD
    positions, series = segment_ids(seg_starts[0], row_length)
    resid = tokens.astype(jnp.float32)
    scale_one = inverse_rms(resid)
    normed_one = (resid * scale_one * gain_attn).astype(jnp.bfloat16)
    gathered_one = lax.all_gather(normed_one, "tp", axis=0, tiled=True)
    query = jnp.dot(gathered_one, full_query, preferred_element_type=jnp.float32).reshape(
        row_length, local_heads, HD
    )
    scaling = softplus_unit / math.sqrt(HD) * jax.nn.softplus(query_scale)
    query_b = (query * scaling).astype(jnp.bfloat16)
    key_b = (
        jnp.dot(gathered_one, full_key, preferred_element_type=jnp.float32)
        .astype(jnp.bfloat16)
        .reshape(row_length, local_heads, HD)
    )
    value_b = (
        jnp.dot(gathered_one, full_value, preferred_element_type=jnp.float32)
        .astype(jnp.bfloat16)
        .reshape(row_length, local_heads, HD)
    )
    mixed, logsum = attend_forward(query_b, key_b, value_b, positions, series, block_rows)
    mixed_b = mixed.astype(jnp.bfloat16)
    attn_part = jnp.dot(mixed_b, full_out, preferred_element_type=jnp.float32)
    middle = resid + lax.psum_scatter(attn_part, "tp", scatter_dimension=0, tiled=True)
    scale_two = inverse_rms(middle)
    normed_two = (middle * scale_two * gain_mlp).astype(jnp.bfloat16)
    wide_up, wide_down = (full_up, full_down)
    mlp_input = lax.all_gather(normed_two, "tp", axis=0, tiled=True)
    upward = jnp.dot(mlp_input, wide_up, preferred_element_type=jnp.float32)
    activated, gelu_back = jax.vjp(jax.nn.gelu, upward)
    hidden_b = activated.astype(jnp.bfloat16)
    mlp_part = jnp.dot(hidden_b, wide_down, preferred_element_type=jnp.float32)
    mlp_sum = lax.psum_scatter(
        mlp_part.astype(jnp.bfloat16), "tp", scatter_dimension=0, tiled=True
    ).astype(jnp.float32)
    result = (middle + mlp_sum).astype(jnp.bfloat16)
    dlower = lax.all_gather(cotangent, "tp", axis=0, tiled=True)
    grad_down_here = jnp.einsum("rf,rd->fd", hidden_b, dlower, preferred_element_type=jnp.float32)
    dhidden = jnp.einsum("rd,fd->rf", dlower, wide_down, preferred_element_type=jnp.float32)
    dupward = gelu_back(dhidden)[0].astype(jnp.bfloat16)
    grad_up_here = jnp.einsum("rd,rf->df", mlp_input, dupward, preferred_element_type=jnp.float32)
    dnorm_part = jnp.einsum("rf,df->rd", dupward, wide_up, preferred_element_type=jnp.float32)
    dnormed_two = lax.psum_scatter(dnorm_part, "tp", scatter_dimension=0, tiled=True)
    grad_up_part, grad_down_part = (grad_up_here, grad_down_here)
    dresid_two, dgain_two = norm_backward(middle, scale_two, gain_mlp, dnormed_two)
    dmiddle = cotangent.astype(jnp.float32) + dresid_two
    dattn = lax.all_gather(dmiddle.astype(jnp.bfloat16), "tp", axis=0, tiled=True)
    grad_out_part = jnp.einsum("rh,rd->hd", mixed_b, dattn, preferred_element_type=jnp.float32)
    dmixed = jnp.einsum("rd,hd->rh", dattn, full_out, preferred_element_type=jnp.float32).astype(
        jnp.bfloat16
    )
    dquery_scaled, dkey, dvalue = attend_backward(
        query_b, key_b, value_b, dmixed, logsum, positions, series, block_rows
    )
    dscaling = jnp.sum(dquery_scaled * query, axis=(0, 1))
    dquery = (dquery_scaled * scaling).astype(jnp.bfloat16).reshape(row_length, local_heads * HD)
    dkey_b = dkey.astype(jnp.bfloat16).reshape(row_length, local_heads * HD)
    dvalue_b = dvalue.astype(jnp.bfloat16).reshape(row_length, local_heads * HD)
    grad_query_part = jnp.einsum(
        "rd,rh->dh", gathered_one, dquery, preferred_element_type=jnp.float32
    )
    grad_key_part = jnp.einsum(
        "rd,rh->dh", gathered_one, dkey_b, preferred_element_type=jnp.float32
    )
    grad_value_part = jnp.einsum(
        "rd,rh->dh", gathered_one, dvalue_b, preferred_element_type=jnp.float32
    )
    dnorm_one_part = jnp.einsum("rh,dh->rd", dquery, full_query, preferred_element_type=jnp.float32)
    dnorm_one_part = dnorm_one_part + jnp.einsum(
        "rh,dh->rd", dkey_b, full_key, preferred_element_type=jnp.float32
    )
    dnorm_one_part = dnorm_one_part + jnp.einsum(
        "rh,dh->rd", dvalue_b, full_value, preferred_element_type=jnp.float32
    )
    dnormed_one = lax.psum_scatter(dnorm_one_part, "tp", scatter_dimension=0, tiled=True)
    dresid_one, dgain_one = norm_backward(resid, scale_one, gain_attn, dnormed_one)
    grad_tokens = dmiddle + dresid_one
    summed = (
        lax.psum_scatter(grad_query_part, "fsdp", scatter_dimension=0, tiled=True),
        lax.psum_scatter(grad_key_part, "fsdp", scatter_dimension=0, tiled=True),
        lax.psum_scatter(grad_value_part, "fsdp", scatter_dimension=0, tiled=True),
        lax.psum_scatter(grad_out_part, "fsdp", scatter_dimension=1, tiled=True),
        lax.psum_scatter(grad_up_part, "fsdp", scatter_dimension=0, tiled=True),
        lax.psum_scatter(grad_down_part, "fsdp", scatter_dimension=1, tiled=True),
    )
    dscale_param = dscaling * (softplus_unit / math.sqrt(HD)) * jax.nn.sigmoid(query_scale)
    grad_gain_attn, grad_gain_mlp, grad_query_scale = lax.psum(
        (dgain_one, dgain_two, dscale_param), ("fsdp", "tp")
    )
    return (
        result,
        grad_tokens,
        grad_gain_attn,
        grad_gain_mlp,
        grad_query_scale,
        summed[0],
        summed[1],
        summed[2],
        summed[3],
        summed[4],
        summed[5],
    )


def spot(place):
    place = lax.rem(place + 16, 8)
    return jnp.where(place < 4, 2 * place, 15 - 2 * place)


RING = (0, 2, 4, 6, 7, 5, 3, 1)
CORES = tuple((i, i ^ 1) for i in range(16))
AROUND = tuple((2 * RING[i], 2 * RING[(i + 1) % 8]) for i in range(8)) + tuple(
    (2 * RING[i] + 1, 2 * RING[(i + 7) % 8] + 1) for i in range(8)
)


def sibling(value):
    return lax.ppermute(value, "fsdp", CORES)


def around(value):
    return lax.ppermute(value, "fsdp", AROUND)


def across(value):
    return lax.ppermute(value, "tp", ((0, 1), (1, 0)))


def where_am_i():
    index = lax.axis_index("fsdp")
    chip, core = index // 2, lax.rem(index, 2)
    place = jnp.where(lax.rem(chip, 2) == 0, chip // 2, 7 - chip // 2)
    return (place, core, 1 - 2 * core)


def ring_gather(own):
    place, core, sign = where_am_i()
    rows, cols = own.shape
    other = sibling(own)
    blocks = [jnp.where(core == 0, jnp.concatenate([own, other]), jnp.concatenate([other, own]))]
    for _ in range(3):
        blocks.append(around(blocks[-1]))
    half = around(lax.dynamic_slice_in_dim(blocks[3], core * rows, rows))
    full = jnp.zeros((16 * rows, cols), own.dtype)

    def put(full, value, chip_place, offset):
        return lax.dynamic_update_slice_in_dim(
            full, value, spot(chip_place) * 2 * rows + offset, axis=0
        )

    full = put(full, blocks[0], place, 0)
    for step in range(1, 4):
        full = put(full, blocks[step], place - sign * step, 0)
        full = put(full, sibling(blocks[step]), place + sign * step, 0)
    full = put(full, half, place + 4, core * rows)
    full = put(full, sibling(half), place + 4, (1 - core) * rows)
    return full


def ring_scatter(grad):
    place, core, sign = where_am_i()
    rows = grad.shape[0] // 16

    def take(chip_place, offset, count):
        return lax.dynamic_slice_in_dim(grad, spot(chip_place) * 2 * rows + offset, count)

    f32 = jnp.float32
    mine, theirs = core * rows, (1 - core) * rows
    first = sibling(
        jnp.concatenate([take(place + 4, theirs, rows), take(place - 3 * sign, 0, 2 * rows)])
    )
    second = sibling(
        jnp.concatenate(
            [
                take(place - 2 * sign, 0, 2 * rows),
                take(place - sign, 0, 2 * rows),
                take(place, theirs, rows),
            ]
        )
    )

    def total(*terms):
        out = terms[0].astype(f32)
        for term in terms[1:]:
            out = out + term.astype(f32)
        return out

    def sent(*terms):
        return total(*terms).astype(jnp.bfloat16)

    came = around(sent(take(place + 4, mine, rows), first[:rows]))
    zero = jnp.zeros_like(came)
    came = jnp.where(
        core == 0, jnp.concatenate([came, zero]), jnp.concatenate([zero, came])
    )
    came = around(sent(take(place + 3 * sign, 0, 2 * rows), first[rows:], came))
    came = around(sent(take(place + 2 * sign, 0, 2 * rows), second[: 2 * rows], came))
    came = around(sent(take(place + sign, 0, 2 * rows), second[2 * rows : 4 * rows], came))
    swapped = sibling(lax.dynamic_slice_in_dim(came, theirs, rows))
    return total(
        take(place, mine, rows),
        second[4 * rows :],
        lax.dynamic_slice_in_dim(came, mine, rows),
        swapped,
    )


def sum_everywhere(value):
    for step in (1, 2, 4, 8):
        value = value + lax.ppermute(value, "fsdp", tuple((i, i ^ step) for i in range(16)))
    return value + across(value)


def dot(a, b, dims):
    return lax.dot_general(a, b, (dims, ((), ())), preferred_element_type=jnp.float32)


def in_order(half, own, other, axis=0):
    return jnp.where(
        half == 0,
        jnp.concatenate([own, other], axis=axis),
        jnp.concatenate([other, own], axis=axis),
    )


def on_slice(
    tokens,
    seg_starts,
    gain_attn,
    gain_mlp,
    query_scale,
    w_query,
    w_key,
    w_value,
    w_out,
    w_up,
    w_down,
    cotangent,
):
    bf16, f32 = jnp.bfloat16, jnp.float32
    half = lax.axis_index("tp")
    rows, width = tokens.shape
    cols = w_query.shape[1]
    length = 2 * rows
    local_heads = cols // HD
    other_tokens = across(tokens)
    w_in = ring_gather(jnp.concatenate([w_query, w_key, w_value], axis=1))
    late = (w_out.T, w_up, w_down.T)
    late_other = across(jnp.concatenate(late, axis=1))
    late = [
        in_order(half, own, late_other[:, i * cols : (i + 1) * cols], axis=1)
        for i, own in enumerate(late)
    ]
    w_late = ring_gather(jnp.concatenate(late, axis=1))
    out_t, up, down_t = (w_late[:, i * width : (i + 1) * width] for i in range(3))

    positions, series = segment_ids(seg_starts[0], length)
    row_tokens = in_order(half, tokens, other_tokens).astype(f32)
    normed_row = (row_tokens * inverse_rms(row_tokens) * gain_attn).astype(bf16)
    proj = dot(w_in, normed_row, ((0,), (1,)))
    scaling = softplus_unit / math.sqrt(HD) * jax.nn.softplus(query_scale)
    query = proj[:cols].reshape(local_heads, HD, length)
    query_b = (query * scaling[None, :, None]).astype(bf16)
    key_b = proj[cols : 2 * cols].astype(bf16).reshape(local_heads, HD, length)
    value_b = proj[2 * cols :].astype(bf16).reshape(local_heads, HD, length)

    allowed = (positions[:, None] <= positions[None, :]) & (series[:, None] == series[None, :])
    scores = jnp.einsum("hdj,hdi->hji", key_b, query_b, preferred_element_type=f32)
    scores = jnp.where(allowed[None], scores, -1e30)
    row_max = jnp.max(scores, axis=1, keepdims=True)
    exponent = jnp.exp(scores - row_max)
    soft = exponent / jnp.sum(exponent, axis=1, keepdims=True)
    soft_b = soft.astype(bf16)
    mixed = jnp.einsum("hdj,hji->hdi", value_b, soft_b, preferred_element_type=f32)
    mixed = mixed.astype(bf16).reshape(cols, length)

    def trade(value):
        mine = lax.dynamic_slice_in_dim(value, half * rows, rows, axis=1)
        came = across(lax.dynamic_slice_in_dim(value, (1 - half) * rows, rows, axis=1))
        return in_order(half, mine, came)

    mixed_b = trade(mixed)
    resid = tokens.astype(f32)
    middle = resid + dot(mixed_b, out_t, ((0,), (1,)))
    scale_two = inverse_rms(middle)
    normed_two = (middle * scale_two * gain_mlp).astype(bf16)
    upward = dot(normed_two, up, ((1,), (0,)))
    activated, gelu_back = jax.vjp(jax.nn.gelu, upward)
    hidden_b = activated.astype(bf16)
    result = (middle + dot(hidden_b, down_t, ((1,), (1,)))).astype(bf16)
    grad_down = dot(cotangent, hidden_b, ((0,), (0,)))
    dhidden = dot(cotangent, down_t, ((1,), (0,)))
    dupward = gelu_back(dhidden)[0].astype(bf16)
    grad_up = dot(normed_two, dupward, ((0,), (0,)))
    dnormed_two = dot(dupward, up, ((1,), (1,)))
    dresid_two, dgain_two = norm_backward(middle, scale_two, gain_mlp, dnormed_two)
    dmiddle = cotangent.astype(f32) + dresid_two
    dattn = dmiddle.astype(bf16)
    grad_out = dot(dattn, mixed_b, ((0,), (1,)))
    dmixed = dot(out_t, dattn, ((0,), (1,))).astype(bf16)
    dlate = ring_scatter(
        jnp.concatenate([grad_out.astype(bf16), grad_up.astype(bf16), grad_down.astype(bf16)], axis=1)
    )

    def trade_back(value):
        mine = lax.dynamic_slice_in_dim(value, half * cols, cols, axis=0)
        came = across(lax.dynamic_slice_in_dim(value, (1 - half) * cols, cols, axis=0))
        return in_order(half, mine, came, axis=1)

    dmixed = trade_back(dmixed).reshape(local_heads, HD, length)
    dsoft = jnp.einsum("hdj,hdi->hji", value_b, dmixed, preferred_element_type=f32)
    inner = jnp.sum(soft * dsoft, axis=1, keepdims=True)
    dscores = (soft * (dsoft - inner)).astype(bf16)
    dquery_s = jnp.einsum("hdj,hji->hdi", key_b, dscores, preferred_element_type=f32)
    dkey = jnp.einsum("hdi,hji->hdj", query_b, dscores, preferred_element_type=f32)
    dvalue = jnp.einsum("hdi,hji->hdj", dmixed, soft_b, preferred_element_type=f32)
    dscaling = jnp.sum(dquery_s * query, axis=(0, 2))
    dquery = (dquery_s * scaling[None, :, None]).astype(bf16)
    dproj = jnp.concatenate(
        [v.astype(bf16).reshape(cols, length) for v in (dquery, dkey, dvalue)], axis=0
    )
    dnormed_row = dot(dproj, w_in, ((0,), (1,))).astype(bf16)
    mine = lax.dynamic_slice_in_dim(dnormed_row, half * rows, rows)
    came = across(lax.dynamic_slice_in_dim(dnormed_row, (1 - half) * rows, rows))
    dnormed_one = mine.astype(f32) + came.astype(f32)
    grad_in = dot(normed_row, dproj, ((0,), (1,))).astype(bf16)
    din = ring_scatter(grad_in)
    dresid_one, dgain_one = norm_backward(resid, inverse_rms(resid), gain_attn, dnormed_one)
    grad_tokens = dmiddle + dresid_one

    def own_half(value):
        keep = lax.dynamic_slice_in_dim(value, half * cols, cols, axis=1)
        came = across(lax.dynamic_slice_in_dim(value, (1 - half) * cols, cols, axis=1).astype(bf16))
        return keep + came.astype(f32)

    wide = dlate.reshape(dlate.shape[0], 3, width)
    keep = lax.dynamic_slice_in_dim(wide, half * cols, cols, axis=2)
    came = across(lax.dynamic_slice_in_dim(wide, (1 - half) * cols, cols, axis=2).astype(bf16))
    dlate = (keep + came.astype(f32)).reshape(dlate.shape[0], 3 * cols)
    dscale_param = dscaling * (softplus_unit / math.sqrt(HD)) * jax.nn.sigmoid(query_scale)
    small = sum_everywhere(
        jnp.stack([dgain_one, dgain_two, jnp.pad(dscale_param, (0, width - HD))])
    )
    return (
        result,
        grad_tokens,
        small[0],
        small[1],
        small[2, :HD],
        din[:, :cols],
        din[:, cols : 2 * cols],
        din[:, 2 * cols :],
        dlate[:, :cols].T,
        dlate[:, cols : 2 * cols],
        dlate[:, 2 * cols :].T,
    )


def solution(mesh):
    body = on_slice if dict(mesh.shape) == {"fsdp": 16, "tp": 2} else on_device
    placed = (
        P(("fsdp", "tp"), None),
        P("fsdp", None),
        P(),
        P(),
        P(),
        P("fsdp", "tp"),
        P("fsdp", "tp"),
        P("fsdp", "tp"),
        P("tp", "fsdp"),
        P("fsdp", "tp"),
        P("tp", "fsdp"),
        P(("fsdp", "tp"), None),
    )
    return jax.shard_map(
        body,
        mesh=mesh,
        in_specs=placed,
        out_specs=(
            P(("fsdp", "tp"), None),
            P(("fsdp", "tp"), None),
            P(),
            P(),
            P(),
            P("fsdp", "tp"),
            P("fsdp", "tp"),
            P("fsdp", "tp"),
            P("tp", "fsdp"),
            P("fsdp", "tp"),
            P("tp", "fsdp"),
        ),
        check_vma=False,
    )
```

```python
import functools
import math

import jax
import jax.numpy as jnp
from jax import lax
from jax.experimental import pallas as pl
from jax.experimental.pallas import tpu as pltpu
from jax.sharding import PartitionSpec as P

HD = 80


epsilon = 1e-06
softplus_unit = 1.442695041


def inverse_rms(values):
    return lax.rsqrt(jnp.mean(values * values, axis=-1, keepdims=True) + epsilon)


def norm_backward(resid, inv_scale, gain, dnormed):
    weighted = dnormed * gain
    cubed = inv_scale * inv_scale * inv_scale
    dresid = inv_scale * weighted - resid * cubed * jnp.mean(
        weighted * resid, axis=-1, keepdims=True
    )
    dgain = jnp.sum(dnormed * resid * inv_scale, axis=0)
    return (dresid, dgain)


def segment_ids(starts, length):
    positions = jnp.arange(length, dtype=jnp.int32)
    inside = (starts[None, :] <= positions[:, None]).astype(jnp.int32)
    return (positions, jnp.sum(inside, axis=1) - 1)


def block_scores(query_blk, block_pos, block_series, key_b, positions, series):
    scores = jnp.einsum("qhd,khd->hqk", query_blk, key_b, preferred_element_type=jnp.float32)
    allowed = (positions[None, :] <= block_pos[:, None]) & (
        series[None, :] == block_series[:, None]
    )
    return jnp.where(allowed[None], scores, -1e30)


def attend_forward(query_b, key_b, value_b, positions, series, block_rows):
    num_blocks = query_b.shape[0] // block_rows
    local_heads = query_b.shape[1]

    def one_block(inputs):
        query_blk, block_pos, block_series = inputs
        scores = block_scores(query_blk, block_pos, block_series, key_b, positions, series)
        row_max = jnp.max(scores, axis=-1, keepdims=True)
        exponent = jnp.exp(scores - row_max)
        total = jnp.sum(exponent, axis=-1, keepdims=True)
        soft_b = (exponent / total).astype(jnp.bfloat16)
        mixed = jnp.einsum("hqk,khd->qhd", soft_b, value_b, preferred_element_type=jnp.float32)
        return (mixed, row_max + jnp.log(total))

    mixed, logsum = lax.map(
        one_block,
        (
            query_b.reshape(num_blocks, block_rows, local_heads, HD),
            positions.reshape(num_blocks, block_rows),
            series.reshape(num_blocks, block_rows),
        ),
    )
    return (mixed.reshape(query_b.shape[0], local_heads * HD), logsum)


def attend_backward(query_b, key_b, value_b, dmixed, logsum, positions, series, block_rows):
    num_blocks = query_b.shape[0] // block_rows
    local_heads = query_b.shape[1]

    def one_block(carry, inputs):
        dkey, dvalue = carry
        query_blk, dmixed_blk, block_pos, block_series, logsum_blk = inputs
        scores = block_scores(query_blk, block_pos, block_series, key_b, positions, series)
        soft = jnp.exp(scores - logsum_blk)
        dsoft = jnp.einsum("qhd,khd->hqk", dmixed_blk, value_b, preferred_element_type=jnp.float32)
        inner = jnp.sum(soft * dsoft, axis=-1, keepdims=True)
        dscores = (soft * (dsoft - inner)).astype(jnp.bfloat16)
        dquery_blk = jnp.einsum("hqk,khd->qhd", dscores, key_b, preferred_element_type=jnp.float32)
        dkey = dkey + jnp.einsum(
            "hqk,qhd->khd", dscores, query_blk, preferred_element_type=jnp.float32
        )
        dvalue = dvalue + jnp.einsum(
            "hqk,qhd->khd",
            soft.astype(jnp.bfloat16),
            dmixed_blk,
            preferred_element_type=jnp.float32,
        )
        return ((dkey, dvalue), dquery_blk)

    zeros = jnp.zeros(key_b.shape, jnp.float32)
    inputs = (
        query_b.reshape(num_blocks, block_rows, local_heads, HD),
        dmixed.reshape(num_blocks, block_rows, local_heads, HD),
        positions.reshape(num_blocks, block_rows),
        series.reshape(num_blocks, block_rows),
        logsum,
    )
    (dkey, dvalue), dquery = lax.scan(one_block, (zeros, zeros), inputs)
    return (dquery.reshape(query_b.shape), dkey, dvalue)


def on_device(
    tokens,
    seg_starts,
    gain_attn,
    gain_mlp,
    query_scale,
    w_query,
    w_key,
    w_value,
    w_out,
    w_up,
    w_down,
    cotangent,
):
    gathered = (
        lax.all_gather(w_query, "fsdp", axis=0, tiled=True),
        lax.all_gather(w_key, "fsdp", axis=0, tiled=True),
        lax.all_gather(w_value, "fsdp", axis=0, tiled=True),
        lax.all_gather(w_out, "fsdp", axis=1, tiled=True),
        lax.all_gather(w_up, "fsdp", axis=0, tiled=True),
        lax.all_gather(w_down, "fsdp", axis=1, tiled=True),
    )
    full_query, full_key, full_value, full_out, full_up, full_down = gathered
    local_rows = tokens.shape[0]
    row_length = local_rows * lax.axis_size("tp")
    block_rows = min(512, row_length)
    local_heads = full_query.shape[1] // HD
    positions, series = segment_ids(seg_starts[0], row_length)
    resid = tokens.astype(jnp.float32)
    scale_one = inverse_rms(resid)
    normed_one = (resid * scale_one * gain_attn).astype(jnp.bfloat16)
    gathered_one = lax.all_gather(normed_one, "tp", axis=0, tiled=True)
    query = jnp.dot(gathered_one, full_query, preferred_element_type=jnp.float32).reshape(
        row_length, local_heads, HD
    )
    scaling = softplus_unit / math.sqrt(HD) * jax.nn.softplus(query_scale)
    query_b = (query * scaling).astype(jnp.bfloat16)
    key_b = (
        jnp.dot(gathered_one, full_key, preferred_element_type=jnp.float32)
        .astype(jnp.bfloat16)
        .reshape(row_length, local_heads, HD)
    )
    value_b = (
        jnp.dot(gathered_one, full_value, preferred_element_type=jnp.float32)
        .astype(jnp.bfloat16)
        .reshape(row_length, local_heads, HD)
    )
    mixed, logsum = attend_forward(query_b, key_b, value_b, positions, series, block_rows)
    mixed_b = mixed.astype(jnp.bfloat16)
    attn_part = jnp.dot(mixed_b, full_out, preferred_element_type=jnp.float32)
    middle = resid + lax.psum_scatter(attn_part, "tp", scatter_dimension=0, tiled=True)
    scale_two = inverse_rms(middle)
    normed_two = (middle * scale_two * gain_mlp).astype(jnp.bfloat16)
    wide_up, wide_down = (full_up, full_down)
    mlp_input = lax.all_gather(normed_two, "tp", axis=0, tiled=True)
    upward = jnp.dot(mlp_input, wide_up, preferred_element_type=jnp.float32)
    activated, gelu_back = jax.vjp(jax.nn.gelu, upward)
    hidden_b = activated.astype(jnp.bfloat16)
    mlp_part = jnp.dot(hidden_b, wide_down, preferred_element_type=jnp.float32)
    mlp_sum = lax.psum_scatter(
        mlp_part.astype(jnp.bfloat16), "tp", scatter_dimension=0, tiled=True
    ).astype(jnp.float32)
    result = (middle + mlp_sum).astype(jnp.bfloat16)
    dlower = lax.all_gather(cotangent, "tp", axis=0, tiled=True)
    grad_down_here = jnp.einsum("rf,rd->fd", hidden_b, dlower, preferred_element_type=jnp.float32)
    dhidden = jnp.einsum("rd,fd->rf", dlower, wide_down, preferred_element_type=jnp.float32)
    dupward = gelu_back(dhidden)[0].astype(jnp.bfloat16)
    grad_up_here = jnp.einsum("rd,rf->df", mlp_input, dupward, preferred_element_type=jnp.float32)
    dnorm_part = jnp.einsum("rf,df->rd", dupward, wide_up, preferred_element_type=jnp.float32)
    dnormed_two = lax.psum_scatter(dnorm_part, "tp", scatter_dimension=0, tiled=True)
    grad_up_part, grad_down_part = (grad_up_here, grad_down_here)
    dresid_two, dgain_two = norm_backward(middle, scale_two, gain_mlp, dnormed_two)
    dmiddle = cotangent.astype(jnp.float32) + dresid_two
    dattn = lax.all_gather(dmiddle.astype(jnp.bfloat16), "tp", axis=0, tiled=True)
    grad_out_part = jnp.einsum("rh,rd->hd", mixed_b, dattn, preferred_element_type=jnp.float32)
    dmixed = jnp.einsum("rd,hd->rh", dattn, full_out, preferred_element_type=jnp.float32).astype(
        jnp.bfloat16
    )
    dquery_scaled, dkey, dvalue = attend_backward(
        query_b, key_b, value_b, dmixed, logsum, positions, series, block_rows
    )
    dscaling = jnp.sum(dquery_scaled * query, axis=(0, 1))
    dquery = (dquery_scaled * scaling).astype(jnp.bfloat16).reshape(row_length, local_heads * HD)
    dkey_b = dkey.astype(jnp.bfloat16).reshape(row_length, local_heads * HD)
    dvalue_b = dvalue.astype(jnp.bfloat16).reshape(row_length, local_heads * HD)
    grad_query_part = jnp.einsum(
        "rd,rh->dh", gathered_one, dquery, preferred_element_type=jnp.float32
    )
    grad_key_part = jnp.einsum(
        "rd,rh->dh", gathered_one, dkey_b, preferred_element_type=jnp.float32
    )
    grad_value_part = jnp.einsum(
        "rd,rh->dh", gathered_one, dvalue_b, preferred_element_type=jnp.float32
    )
    dnorm_one_part = jnp.einsum("rh,dh->rd", dquery, full_query, preferred_element_type=jnp.float32)
    dnorm_one_part = dnorm_one_part + jnp.einsum(
        "rh,dh->rd", dkey_b, full_key, preferred_element_type=jnp.float32
    )
    dnorm_one_part = dnorm_one_part + jnp.einsum(
        "rh,dh->rd", dvalue_b, full_value, preferred_element_type=jnp.float32
    )
    dnormed_one = lax.psum_scatter(dnorm_one_part, "tp", scatter_dimension=0, tiled=True)
    dresid_one, dgain_one = norm_backward(resid, scale_one, gain_attn, dnormed_one)
    grad_tokens = dmiddle + dresid_one
    summed = (
        lax.psum_scatter(grad_query_part, "fsdp", scatter_dimension=0, tiled=True),
        lax.psum_scatter(grad_key_part, "fsdp", scatter_dimension=0, tiled=True),
        lax.psum_scatter(grad_value_part, "fsdp", scatter_dimension=0, tiled=True),
        lax.psum_scatter(grad_out_part, "fsdp", scatter_dimension=1, tiled=True),
        lax.psum_scatter(grad_up_part, "fsdp", scatter_dimension=0, tiled=True),
        lax.psum_scatter(grad_down_part, "fsdp", scatter_dimension=1, tiled=True),
    )
    dscale_param = dscaling * (softplus_unit / math.sqrt(HD)) * jax.nn.sigmoid(query_scale)
    grad_gain_attn, grad_gain_mlp, grad_query_scale = lax.psum(
        (dgain_one, dgain_two, dscale_param), ("fsdp", "tp")
    )
    return (
        result,
        grad_tokens,
        grad_gain_attn,
        grad_gain_mlp,
        grad_query_scale,
        summed[0],
        summed[1],
        summed[2],
        summed[3],
        summed[4],
        summed[5],
    )


BF16, F32 = jnp.bfloat16, jnp.float32
RING = (0, 2, 4, 6, 7, 5, 3, 1)
CORES = tuple((i, i ^ 1) for i in range(16))
AROUND = tuple((2 * RING[i], 2 * RING[(i + 1) % 8]) for i in range(8)) + tuple(
    (2 * RING[i] + 1, 2 * RING[(i + 7) % 8] + 1) for i in range(8)
)
VMEM = pl.BlockSpec(memory_space=pltpu.VMEM)
HELD = pl.BlockSpec(memory_space=pltpu.VMEM)
LIMIT = 30 * 2**20
UNROLL = (4, 8)
SMEM = pl.BlockSpec(memory_space=pltpu.SMEM)
ANY = pl.BlockSpec(memory_space=pl.ANY)
LEAVE = (9, 6, 7, 4, 5, 2, 3, 1)
STAY = (8, 14, 15, 12, 13, 10, 11, 0)
STEPS = (1, 2, 2, 2, 1)
FAR_STEPS = (1, 2, 2, 3)


def sibling(value):
    return lax.ppermute(value, "fsdp", CORES)


def around(value):
    return lax.ppermute(value, "fsdp", AROUND)


def across(value):
    return lax.ppermute(value, "tp", ((0, 1), (1, 0)))


def arrival_order(rows):
    index = lax.axis_index("fsdp")
    chip, core = index // 2, lax.rem(index, 2)
    place = jnp.where(lax.rem(chip, 2) == 0, chip // 2, 7 - chip // 2)
    sign = 1 - 2 * core

    def shard(step, which):
        at = lax.rem(place + step + 16, 8)
        return 2 * jnp.where(at < 4, 2 * at, 15 - 2 * at) + which

    order = [shard(0, core), shard(0, 1 - core)]
    for step in (1, 2, 3):
        order += [shard(-step * sign, core), shard(-step * sign, 1 - core)]
    order += [shard(4, core), shard(4, 1 - core)]
    for step in (1, 2, 3):
        order += [shard(step * sign, 1 - core), shard(step * sign, core)]
    return jnp.stack([rows * o for o in order] + [lax.axis_index("tp")]).astype(jnp.int32)


def after(value, *others):
    return lax.optimization_barrier((value, *others))[0]


def pack_kernel(query, key, value, out, up, down, early, late):
    cols = query.shape[1]
    for n, ref in enumerate((query, key, value)):
        early[:, n * cols : (n + 1) * cols] = ref[...]
    late[:, :cols] = out[...]
    late[:, cols : 2 * cols] = up[...]
    late[:, 2 * cols :] = down[...]


def all_after(values, *others):
    return lax.optimization_barrier((*values, *others))[: len(values)]


def ring_gather(early, late, tokens, prepare):
    rows = early.shape[0]
    first = [early, sibling(early)]
    here = [late, sibling(after(late, first[1]))]
    other_tokens = across(tokens)
    there = [across(after(late, other_tokens))]
    first.append(around(jnp.concatenate(first)))
    here.append(around(jnp.concatenate(here)))
    first.append(around(after(first[2], other_tokens)))
    here.append(around(here[2]))
    there.append(across(here[2]))
    first.append(around(after(first[3], there[0])))
    here.append(around(here[3]))
    there.append(across(here[3]))
    prepared = prepare(other_tokens)
    first.append(around(after(first[4][:rows], prepared, there[1])))
    here.append(around(here[4][:rows]))
    there.append(across(here[4]))
    there.append(across(here[5]))
    first += [sibling(after(first[5], here[5]))] + [sibling(first[n]) for n in (2, 3, 4)]
    return (first, here, there, prepared, other_tokens)


def swap_late(here, there, *wait):
    there = [there[0], sibling(there[0])] + there[1:]
    return [
        got + [sibling(after(got[n], *wait)) for n in (5, 2, 3, 4)] for got in (here, there)
    ]


def total(*terms):
    out = terms[0].astype(F32)
    for term in terms[1:]:
        out = out + term.astype(F32)
    return out


class Scatter:
    def __init__(self, parts, far=None, note=None):
        self.came_from = [sibling(part) for part in parts[:5]]
        self.stay = parts[5:]
        self.far = far
        self.rows, self.cols = self.stay[0].shape
        self.came = None
        self.note = note
        self.notes = []

    def step(self, number, *wait):
        terms = [self.stay[number], self.came_from[number]]
        rows = STEPS[number] * self.rows
        note = self.note is not None
        if self.far is not None:
            terms.append(self.far[number])
        if self.came is not None:
            terms.append(self.came)
        elif note:
            terms.append(self.note)
        if number == 0 and note:
            body = first_kernel
        else:
            body = functools.partial(add_kernel, number, note)
        out = struct(rows + (16 if note else 0), self.cols)
        sent = call(body, terms, [HELD] * len(terms), [(out, HELD)], [], 10**6)[0]
        self.sent = sent
        came = around(after(sent, *wait) if wait else sent)
        if note:
            self.notes.append(came[rows:])
        self.came = came
        return came

    def finish(self):
        rows = self.rows
        came = self.came
        terms = [self.stay[4], self.came_from[4], came[rows : 2 * rows], sibling(came[:rows])]
        if self.far is not None:
            terms.append(self.far[4])
        return total(*terms)


def dot(a, b, dims):
    return lax.dot_general(a, b, (dims, ((), ())), preferred_element_type=F32)


NN, NT = ((1,), (0,)), ((1,), (1,))


def put_shards(order, pieces, target, sems):
    rows = pieces[0].shape[0]
    copies = []
    for n, piece in enumerate(pieces[:2]):
        to = pl.ds(pl.multiple_of(order[n], 16), rows)
        copies.append(load(piece, target.at[to, :], sems.at[n]))
    n = 2
    for piece in pieces[2:]:
        for part in range(piece.shape[0] // rows):
            to = pl.ds(pl.multiple_of(order[n], 16), rows)
            target[to, :] = piece[part * rows : (part + 1) * rows, :]
            n += 1
    wait_all(copies)


def load(source, target, sem):
    copy = pltpu.make_async_copy(source, target, sem)
    copy.start()
    return copy


def wait_all(copies):
    for copy in copies:
        copy.wait()


def allowed_bias(starts, bias):
    length = bias.shape[0]
    key_pos = lax.broadcasted_iota(jnp.int32, (length, 1), 0)
    query_pos = lax.broadcasted_iota(jnp.int32, (1, length), 1)
    key_series = jnp.zeros((length, 1), jnp.int32)
    query_series = jnp.zeros((1, length), jnp.int32)
    for n in range(starts.shape[1]):
        key_series += (starts[0, n] <= key_pos).astype(jnp.int32)
        query_series += (starts[0, n] <= query_pos).astype(jnp.int32)
    allowed = (key_pos <= query_pos) & (key_series == query_series)
    bias[...] = jnp.where(allowed, 0.0, -1e30).astype(F32)


def attend_kernel(heads, order, starts, scaling, normed, *rest):
    pieces, rest = rest[:10], rest[10:]
    keep, send, logsum, proj_out, weights_out, proj_t, weights, bias, scores, mixed, sems = rest
    cols = heads * HD
    length = normed.shape[0]
    allowed_bias(starts, bias)
    put_shards(order, pieces, weights, sems)
    stores = [load(weights, weights_out, sems.at[2])]
    for n in range(3):
        part = dot(normed[...], weights[:, n * cols : (n + 1) * cols], NN)
        if n == 0:
            part = part * scaling[...]
        proj_t[n * cols : (n + 1) * cols, :] = part.astype(BF16).T
    stores.append(load(proj_t, proj_out, sems.at[3]))
    blocks = ((0, length // 2), (length // 2, length))

    def rows(n, h):
        return pl.ds(pl.multiple_of(n * cols + h * HD, 16), HD)

    def one_head(h, slot):
        query = proj_t[rows(0, h), :]
        key = proj_t[rows(1, h), :].T
        value = proj_t[rows(2, h), :]
        for start, stop in blocks:
            scores[slot, :stop, start:stop] = dot(key[:stop], query[:, start:stop], NN)
        for start, stop in blocks:
            part = scores[slot, :stop, start:stop] + bias[:stop, start:stop]
            row_max = jnp.max(part, axis=0, keepdims=True)
            exponent = jnp.exp(part - row_max)
            total = jnp.sum(exponent, axis=0, keepdims=True)
            soft_b = (exponent * (1.0 / total)).astype(BF16)
            mixed[rows(0, h), start:stop] = dot(value[:, :stop], soft_b, NN).astype(BF16)
            logsum[h, :, start:stop] = row_max + jnp.log(total)

    @pl.loop(0, heads // UNROLL[0])
    def _(block):
        for n in range(UNROLL[0]):
            one_head(block * UNROLL[0] + n, n)

    half = order[16]
    low, high = mixed[:, : length // 2], mixed[:, length // 2 :]
    keep[...] = jnp.where(half == 0, low, high)
    send[...] = jnp.where(half == 0, high, low)
    wait_all(stores)


def assemble_kernel(order, *rest):
    here, there, (weights, sems) = rest[:10], rest[10:20], rest[20:]
    put_shards(order, here, weights.at[0], sems)
    put_shards(order, there, weights.at[1], sems)


def middle_kernel(
    tokens, cot, gain, keep, came, weights,
    dkeep, dsend, hidden_o, dup_o, normed_o, dattn_o, mixed_o, middle_o, dgain_o, dmiddle_out,
    dhidden, dmiddle_o, sem,
):
    cols = keep.shape[0]
    out, up, down = (slice(n * cols, (n + 1) * cols) for n in range(3))

    def half(n):
        return pl.ds(pl.multiple_of(n * cols, 128), cols)

    mixed_o[:, :cols] = keep[...].T
    mixed_o[:, cols:] = came[...].T
    middle_o[...] = tokens[...].astype(F32)

    @pl.loop(0, 2)
    def _(n):
        middle_o[...] += dot(mixed_o[:, half(n)], weights[n, :, out], NT)
        dhidden[:, half(n)] = dot(cot[...], weights[n, :, down], NN)

    middle = middle_o[...]
    scale = lax.rsqrt(jnp.mean(middle * middle, axis=-1, keepdims=True) + epsilon)
    normed_o[...] = (middle * scale * gain[...]).astype(BF16)

    @pl.loop(0, 2)
    def _(n):
        u = dot(normed_o[...], weights[n, :, up], NN)
        root = math.sqrt(2.0 / math.pi)
        square = u * u
        tanh = jnp.tanh(root * u * (1.0 + 0.044715 * square))
        gate = 0.5 * (1.0 + tanh)
        hidden_o[:, half(n)] = (u * gate).astype(BF16)
        slope = gate + 0.5 * u * (1.0 - tanh * tanh) * (root * (1.0 + 3 * 0.044715 * square))
        dup_o[:, half(n)] = (dhidden[:, half(n)] * slope).astype(BF16)

    dmiddle_o[...] = jnp.zeros_like(dmiddle_o)

    @pl.loop(0, 2)
    def _(n):
        dmiddle_o[...] += dot(dup_o[:, half(n)], weights[n, :, up], NT)

    dnormed = dmiddle_o[...]
    middle = middle_o[...]
    dgain_o[...] = jnp.sum(dnormed * middle * scale, axis=0, keepdims=True)
    weighted = dnormed * gain[...]
    mean = jnp.mean(weighted * middle, axis=-1, keepdims=True)
    dmiddle = cot[...].astype(F32) + scale * weighted - middle * (scale * scale * scale * mean)
    dmiddle_o[...] = dmiddle
    store = load(dmiddle_o, dmiddle_out, sem)
    dattn_o[...] = dmiddle.astype(BF16)
    for n, ref in enumerate((dkeep, dsend)):
        ref[...] = dot(dattn_o[...], weights[n, :, out], NN).astype(BF16).T
    store.wait()


def by_arrival(order, source_t, target, rows):
    for n, which in enumerate(LEAVE + STAY):
        target[n * rows : (n + 1) * rows, :] = source_t[
            pl.ds(pl.multiple_of(order[which], 16), rows), :
        ]


def split_rows(steps, rows, at=0):
    out = []
    for count in steps:
        out.append(slice(at, at + count * rows))
        at += count * rows
    return out


def late_grads_kernel(order, hidden, dup, normed, dattn, mixed, middle, weights, cot, *rest):
    outs, (grads, result, left_t, left, sems) = rest[:19], rest[19:]
    cols = dup.shape[1] // 2
    rows = dup.shape[1] // 16
    pairs = ((dattn, mixed), (normed, dup), (cot, hidden))
    for n, (a, _) in enumerate(pairs):
        left_t[...] = a[...].T
        by_arrival(order, left_t, left.at[n], rows)
    stores = []
    for leaves in range(2):
        top = leaves * 8 * rows
        part = slice(top, top + 8 * rows)
        for side, steps, start in ((1, FAR_STEPS, 10), (0, STEPS, 0)):
            for n, (_, b) in enumerate(pairs):
                grads[side, part, n * cols : (n + 1) * cols] = dot(
                    left[n, part, :], b[:, side * cols : (side + 1) * cols], NN
                ).astype(BF16)
            start += leaves * len(steps)
            for k, at in enumerate(split_rows(steps, rows, top)):
                stores.append(load(grads.at[side, at, :], outs[start + k], sems.at[start + k]))
    total = middle[...]
    for side in range(2):
        at = slice(side * cols, (side + 1) * cols)
        total = total + dot(hidden[:, at], weights[side, :, 2 * cols :], NT)
    result[...] = total.astype(BF16)
    stores.append(load(result, outs[18], sems.at[18]))
    wait_all(stores)


def attend_back_kernel(
    heads, order, starts, scaling_col, keep, came, logsum, proj_in, weights_in, tokens_in, other_in,
    dscaling, dgain, dproj_out, keep_out, send_out,
    weights, proj_t, bias, dmixed, dproj_t, scores, dsofts, dproj, kept, sent, tokens, sems,
):
    fetch = load(proj_in, proj_t, sems.at[0])
    fetch_late = [
        load(weights_in, weights, sems.at[1]),
        load(tokens_in, tokens.at[0], sems.at[2]),
        load(other_in, tokens.at[1], sems.at[3]),
    ]
    cols = heads * HD
    length = proj_t.shape[1]
    rows = length // 2
    allowed_bias(starts, bias)
    half = order[16]
    dmixed[:, :rows] = jnp.where(half == 0, keep[...], came[...])
    dmixed[:, rows:] = jnp.where(half == 0, came[...], keep[...])
    fetch.wait()
    dscaling[...] = jnp.zeros_like(dscaling)

    def place(n, h):
        return pl.ds(pl.multiple_of(n * cols + h * HD, 16), HD)

    def one_head(h, slot):
        query = proj_t[place(0, h), :]
        key_t = proj_t[place(1, h), :]
        key = key_t.T
        value = proj_t[place(2, h), :].T
        grad = dmixed[place(0, h), :]
        for start, stop in ((0, rows), (rows, length)):
            scores[slot, :stop, start:stop] = dot(key[:stop], query[:, start:stop], NN)
            dsofts[slot, :stop, start:stop] = dot(value[:stop], grad[:, start:stop], NN)
        parts = []
        for start, stop in ((rows, length), (0, rows)):
            soft = scores[slot, :stop, start:stop] + bias[:stop, start:stop]
            soft = jnp.exp(soft - logsum[h, :, start:stop])
            dsoft = dsofts[slot, :stop, start:stop]
            inner = jnp.sum(soft * dsoft, axis=0, keepdims=True)
            dscores = (soft * (dsoft - inner)).astype(BF16)
            dquery = dot(key_t[:, :stop], dscores, NN)
            dscaling[...] += jnp.sum(
                dquery * query[:, start:stop].astype(F32), axis=1, keepdims=True
            )
            dproj_t[place(0, h), start:stop] = (dquery * scaling_col[...]).astype(BF16)
            parts.append(
                (dot(dscores, query[:, start:stop], NT), dot(soft.astype(BF16), grad[:, start:stop], NT))
            )
        for n in range(2):
            both = jnp.concatenate([parts[0][n][:rows] + parts[1][n], parts[0][n][rows:]], axis=0)
            dproj_t[place(n + 1, h), :] = both.astype(BF16).T

    @pl.loop(0, heads // UNROLL[1])
    def _(block):
        for n in range(UNROLL[1]):
            one_head(block * UNROLL[1] + n, n % 2)

    dproj[...] = dproj_t[...].T
    stores = [load(dproj, dproj_out, sems.at[4])]
    wait_all(fetch_late)
    parts = []
    total = jnp.zeros(dgain.shape, F32)
    for n in range(2):
        part = dot(dproj[n * rows : (n + 1) * rows, :], weights[...], NT)
        resid = jnp.where(half == n, tokens[0], tokens[1]).astype(F32)
        scale = lax.rsqrt(jnp.mean(resid * resid, axis=-1, keepdims=True) + epsilon)
        total = total + jnp.sum(part * resid * scale, axis=0, keepdims=True)
        parts.append(part)
    dgain[...] = total
    sent[...] = jnp.where(half == 0, parts[1], parts[0]).astype(BF16)
    stores.append(load(sent, send_out, sems.at[5]))
    kept[...] = jnp.where(half == 0, parts[0], parts[1])
    stores.append(load(kept, keep_out, sems.at[6]))
    wait_all(stores)


def early_grads_kernel(order, normed, dproj_in, *rest):
    outs, (dproj, grads, left_t, left, sems) = rest[:10], rest[10:]
    fetch = load(dproj_in, dproj, sems.at[10])
    rows = normed.shape[1] // 16
    left_t[...] = normed[...].T
    by_arrival(order, left_t, left, rows)
    fetch.wait()
    stores = []
    for leaves in range(2):
        top = leaves * 8 * rows
        part = slice(top, top + 8 * rows)
        grads[part, :] = dot(left[part, :], dproj[...], NN).astype(BF16)
        for k, at in enumerate(split_rows(STEPS, rows, top)):
            n = 5 * leaves + k
            stores.append(load(grads.at[at, :], outs[n], sems.at[n]))
    wait_all(stores)


def first_kernel(stay, came, note, out):
    rows = stay.shape[0]
    out[:rows, :] = (stay[...].astype(F32) + came[...].astype(F32)).astype(BF16)
    out[rows:, :] = note[...]


def add_kernel(number, note, *rest):
    *terms, out = rest
    rows = terms[0].shape[0]
    late = terms.pop() if number > 0 else None
    part = terms[0][...].astype(F32)
    for term in terms[1:]:
        part = part + term[...].astype(F32)
    if number == 1:
        half = rows // 2
        out[:half, :] = part[:half].astype(BF16)
        out[half:rows, :] = (part[half:] + late[:half, :].astype(F32)).astype(BF16)
    else:
        if late is not None:
            part = part + late[:rows, :].astype(F32)
        out[:rows, :] = part.astype(BF16)
    if note:
        out[rows:, :] = late[late.shape[0] - 16 :, :]


def pair_kernel(one, other, out):
    out[...] = (one[...].astype(F32) + other[...].astype(F32)).astype(BF16)


def struct(*shape, kind=BF16):
    return jax.ShapeDtypeStruct(shape, kind)


def call(body, inputs, spaces, outputs, scratch, flops):
    place = {id(HELD): pltpu.VMEM, id(ANY): pltpu.HBM, id(VMEM): pltpu.HBM}
    inputs = [
        pltpu.with_memory_space_constraint(value, place[id(space)]) if id(space) in place else value
        for value, space in zip(inputs, spaces)
    ]
    return pl.pallas_call(
        body,
        out_shape=[place[id(space)](out.shape, out.dtype) for out, space in outputs],
        in_specs=[VMEM if space is HELD else space for space in spaces],
        out_specs=[VMEM if space is HELD else space for _, space in outputs],
        scratch_shapes=scratch,
        compiler_params=pltpu.CompilerParams(vmem_limit_bytes=LIMIT),
        cost_estimate=pl.CostEstimate(flops=flops * 4, bytes_accessed=2**22, transcendentals=0),
    )(*inputs)


def in_order(half, own, other, axis=0):
    return jnp.where(
        half == 0,
        jnp.concatenate([own, other], axis=axis),
        jnp.concatenate([other, own], axis=axis),
    )


def on_slice(
    tokens,
    seg_starts,
    gain_attn,
    gain_mlp,
    query_scale,
    w_query,
    w_key,
    w_value,
    w_out,
    w_up,
    w_down,
    cotangent,
):
    half = lax.axis_index("tp")
    rows, width = tokens.shape
    shard, cols = w_query.shape
    length = 2 * rows
    heads = cols // HD
    dma = pltpu.SemaphoreType.DMA
    order = arrival_order(shard)
    early, late = call(
        pack_kernel,
        [w_query, w_key, w_value, w_out.T, w_up, w_down.T],
        [VMEM] * 6,
        [(struct(shard, 3 * cols), VMEM)] * 2,
        [],
        10**6,
    )

    def prepare(other_tokens):
        row_tokens = in_order(half, tokens, other_tokens).astype(F32)
        return (row_tokens * inverse_rms(row_tokens) * gain_attn).astype(BF16)

    first, here, there, normed, other_tokens = ring_gather(early, late, tokens, prepare)
    scaling = softplus_unit / math.sqrt(HD) * jax.nn.softplus(query_scale)
    keep, send, logsum, proj_t, w_in = call(
        functools.partial(attend_kernel, heads),
        [after(order, there[2]), seg_starts, jnp.tile(scaling, heads)[None, :], normed]
        + first,
        [SMEM] * 2 + [HELD] * 2 + [ANY] * 2 + [HELD] * 8,
        [
            (struct(cols, rows), HELD),
            (struct(cols, rows), HELD),
            (struct(heads, 1, length, kind=F32), HELD),
            (struct(3 * cols, length), ANY),
            (struct(width, 3 * cols), ANY),
        ],
        [
            pltpu.VMEM((3 * cols, length), BF16),
            pltpu.VMEM((width, 3 * cols), BF16),
            pltpu.VMEM((length, length), F32),
            pltpu.VMEM((UNROLL[0], length, length), F32),
            pltpu.VMEM((cols, length), BF16),
            dma((4,)),
        ],
        8 * 10**9,
    )
    came = across(send)
    here, there = swap_late(here, there, logsum)
    w_late = call(
        assemble_kernel,
        [after(order, came), *here, *there],
        [SMEM] + ([ANY] * 2 + [HELD] * 8) * 2,
        [(struct(2, width, 3 * cols), HELD)],
        [dma((2,))],
        10**6,
    )[0]
    act = struct(rows, width)
    dkeep, dsend, *saved, dgain_two, dmiddle = call(
        middle_kernel,
        [tokens, cotangent, gain_mlp[None, :], keep, came, w_late],
        [HELD] * 6,
        [(struct(cols, rows), HELD)] * 2
        + [(act, HELD)] * 5
        + [
            (struct(rows, width, kind=F32), HELD),
            (struct(1, width, kind=F32), HELD),
            (struct(rows, width, kind=F32), ANY),
        ],
        [pltpu.VMEM((rows, width), F32), pltpu.VMEM((rows, width), F32), dma],
        8 * 10**9,
    )
    dcame = across(dsend)
    *parts, result = call(
        late_grads_kernel,
        [order, *saved, w_late, cotangent],
        [SMEM] + [HELD] * 8,
        [(struct(n * shard, 3 * cols), ANY) for n in STEPS * 2 + FAR_STEPS * 2] + [(act, ANY)],
        [
            pltpu.VMEM((2, width, 3 * cols), BF16),
            pltpu.VMEM((rows, width), BF16),
            pltpu.VMEM((width, rows), BF16),
            pltpu.VMEM((3, width, rows), BF16),
            dma((19,)),
        ],
        6 * 10**9,
    )
    *parts, result = all_after((*parts, result), dcame)
    far = []
    for n, steps in enumerate(FAR_STEPS):
        pair = [parts[14 + n], sibling(parts[10 + n])]
        sent = call(pair_kernel, pair, [HELD] * 2, [(struct(steps * shard, 3 * cols), HELD)], [], 10**6)
        far.append(across(sent[0]))
    far_last = far.pop()
    far += [far_last[: 2 * shard], far_last[2 * shard :]]
    late_sum = Scatter(parts[:10], far)
    late_one = late_sum.step(0)
    dscaling, dgain_one, dproj, dnormed, dnormed_send = call(
        functools.partial(attend_back_kernel, heads),
        [
            after(order, late_sum.came_from[0]),
            seg_starts,
            scaling[:, None],
            dkeep,
            dcame,
            logsum,
            proj_t,
            w_in,
            tokens,
            other_tokens,
        ],
        [SMEM] * 2 + [HELD] * 4 + [ANY] * 4,
        [
            (struct(HD, 1, kind=F32), HELD),
            (struct(1, width, kind=F32), HELD),
            (struct(length, 3 * cols), ANY),
            (struct(rows, width, kind=F32), ANY),
            (act, ANY),
        ],
        [
            pltpu.VMEM((width, 3 * cols), BF16),
            pltpu.VMEM((3 * cols, length), BF16),
            pltpu.VMEM((length, length), F32),
            pltpu.VMEM((cols, length), BF16),
            pltpu.VMEM((3 * cols, length), BF16),
            pltpu.VMEM((2, length, length), F32),
            pltpu.VMEM((2, length, length), F32),
            pltpu.VMEM((length, 3 * cols), BF16),
            pltpu.VMEM((rows, width), F32),
            pltpu.VMEM((rows, width), BF16),
            pltpu.VMEM((2, rows, width), BF16),
            dma((7,)),
        ],
        12 * 10**9,
    )
    dscaling, dgain_one, dproj, dnormed, dnormed_send = all_after(
        (dscaling, dgain_one, dproj, dnormed, dnormed_send), *far[:2]
    )
    dscale_param = (
        dscaling[:, 0] / scaling * (softplus_unit / math.sqrt(HD)) * jax.nn.sigmoid(query_scale)
    )
    note = jnp.concatenate(
        [
            jnp.concatenate([dgain_one, jnp.pad(dscale_param[None, :], ((0, 0), (0, cols - HD)))], axis=1),
            jnp.pad(dgain_two, ((0, 0), (0, cols))),
        ]
    )
    parts = call(
        early_grads_kernel,
        [order, normed, dproj],
        [SMEM, HELD, ANY],
        [(struct(n * shard, 3 * cols), ANY) for n in STEPS + STEPS],
        [
            pltpu.VMEM((length, 3 * cols), BF16),
            pltpu.VMEM((width, 3 * cols), BF16),
            pltpu.VMEM((width, length), BF16),
            pltpu.VMEM((width, length), BF16),
            dma((11,)),
        ],
        5 * 10**9,
    )
    note = note + sibling(after(note, parts[1]))
    high = lax.reduce_precision(note, 8, 7)
    coded = jnp.concatenate([high, note - high, jnp.zeros((12, 3 * cols), F32)]).astype(BF16)
    parts = all_after(parts, late_one, far[2])
    late_two = late_sum.step(1)
    early_sum = Scatter(parts, note=coded)
    early_sum.step(0)
    late_three = late_sum.step(2)
    dnormed = dnormed + across(dnormed_send).astype(F32)
    resid = tokens.astype(F32)
    dresid_one, _ = norm_backward(resid, inverse_rms(resid), gain_attn, dnormed)
    early_sum.step(1, late_two)
    late_four = late_sum.step(3)
    early_sum.step(2, late_three)
    early_sum.step(3, late_four)
    dlate = late_sum.finish()
    din = early_sum.finish()
    mine = early_sum.notes
    core = lax.rem(lax.axis_index("fsdp"), 2)
    heard = total(*mine[:3]) + jnp.where(core == 0, 1.0, 0.0) * mine[3].astype(F32)
    heard = heard[:2] + heard[2:4]
    heard = heard + sibling(heard)
    small = note + heard
    small = small + across(small)
    return (
        result,
        dmiddle + dresid_one,
        small[0, :width],
        small[1, :width],
        small[0, width : width + HD],
        din[:, :cols],
        din[:, cols : 2 * cols],
        din[:, 2 * cols :],
        dlate[:, :cols].T,
        dlate[:, cols : 2 * cols],
        dlate[:, 2 * cols :].T,
    )


def solution(mesh):
    body = on_slice if dict(mesh.shape) == {"fsdp": 16, "tp": 2} else on_device
    placed = (
        P(("fsdp", "tp"), None),
        P("fsdp", None),
        P(),
        P(),
        P(),
        P("fsdp", "tp"),
        P("fsdp", "tp"),
        P("fsdp", "tp"),
        P("tp", "fsdp"),
        P("fsdp", "tp"),
        P("tp", "fsdp"),
        P(("fsdp", "tp"), None),
    )
    return jax.shard_map(
        body,
        mesh=mesh,
        in_specs=placed,
        out_specs=(
            P(("fsdp", "tp"), None),
            P(("fsdp", "tp"), None),
            P(),
            P(),
            P(),
            P("fsdp", "tp"),
            P("fsdp", "tp"),
            P("fsdp", "tp"),
            P("tp", "fsdp"),
            P("fsdp", "tp"),
            P("tp", "fsdp"),
        ),
        check_vma=False,
    )
```

```python
import functools
import math

import jax
import jax.numpy as jnp
from jax import lax
from jax.experimental import pallas as pl
from jax.experimental.pallas import tpu as pltpu
from jax.sharding import PartitionSpec as P

HD = 80


epsilon = 1e-06
softplus_unit = 1.442695041


def inverse_rms(values):
    return lax.rsqrt(jnp.mean(values * values, axis=-1, keepdims=True) + epsilon)


def norm_backward(resid, inv_scale, gain, dnormed):
    weighted = dnormed * gain
    cubed = inv_scale * inv_scale * inv_scale
    dresid = inv_scale * weighted - resid * cubed * jnp.mean(
        weighted * resid, axis=-1, keepdims=True
    )
    dgain = jnp.sum(dnormed * resid * inv_scale, axis=0)
    return (dresid, dgain)


def segment_ids(starts, length):
    positions = jnp.arange(length, dtype=jnp.int32)
    inside = (starts[None, :] <= positions[:, None]).astype(jnp.int32)
    return (positions, jnp.sum(inside, axis=1) - 1)


def block_scores(query_blk, block_pos, block_series, key_b, positions, series):
    scores = jnp.einsum("qhd,khd->hqk", query_blk, key_b, preferred_element_type=jnp.float32)
    allowed = (positions[None, :] <= block_pos[:, None]) & (
        series[None, :] == block_series[:, None]
    )
    return jnp.where(allowed[None], scores, -1e30)


def attend_forward(query_b, key_b, value_b, positions, series, block_rows):
    num_blocks = query_b.shape[0] // block_rows
    local_heads = query_b.shape[1]

    def one_block(inputs):
        query_blk, block_pos, block_series = inputs
        scores = block_scores(query_blk, block_pos, block_series, key_b, positions, series)
        row_max = jnp.max(scores, axis=-1, keepdims=True)
        exponent = jnp.exp(scores - row_max)
        total = jnp.sum(exponent, axis=-1, keepdims=True)
        soft_b = (exponent / total).astype(jnp.bfloat16)
        mixed = jnp.einsum("hqk,khd->qhd", soft_b, value_b, preferred_element_type=jnp.float32)
        return (mixed, row_max + jnp.log(total))

    mixed, logsum = lax.map(
        one_block,
        (
            query_b.reshape(num_blocks, block_rows, local_heads, HD),
            positions.reshape(num_blocks, block_rows),
            series.reshape(num_blocks, block_rows),
        ),
    )
    return (mixed.reshape(query_b.shape[0], local_heads * HD), logsum)


def attend_backward(query_b, key_b, value_b, dmixed, logsum, positions, series, block_rows):
    num_blocks = query_b.shape[0] // block_rows
    local_heads = query_b.shape[1]

    def one_block(carry, inputs):
        dkey, dvalue = carry
        query_blk, dmixed_blk, block_pos, block_series, logsum_blk = inputs
        scores = block_scores(query_blk, block_pos, block_series, key_b, positions, series)
        soft = jnp.exp(scores - logsum_blk)
        dsoft = jnp.einsum("qhd,khd->hqk", dmixed_blk, value_b, preferred_element_type=jnp.float32)
        inner = jnp.sum(soft * dsoft, axis=-1, keepdims=True)
        dscores = (soft * (dsoft - inner)).astype(jnp.bfloat16)
        dquery_blk = jnp.einsum("hqk,khd->qhd", dscores, key_b, preferred_element_type=jnp.float32)
        dkey = dkey + jnp.einsum(
            "hqk,qhd->khd", dscores, query_blk, preferred_element_type=jnp.float32
        )
        dvalue = dvalue + jnp.einsum(
            "hqk,qhd->khd",
            soft.astype(jnp.bfloat16),
            dmixed_blk,
            preferred_element_type=jnp.float32,
        )
        return ((dkey, dvalue), dquery_blk)

    zeros = jnp.zeros(key_b.shape, jnp.float32)
    inputs = (
        query_b.reshape(num_blocks, block_rows, local_heads, HD),
        dmixed.reshape(num_blocks, block_rows, local_heads, HD),
        positions.reshape(num_blocks, block_rows),
        series.reshape(num_blocks, block_rows),
        logsum,
    )
    (dkey, dvalue), dquery = lax.scan(one_block, (zeros, zeros), inputs)
    return (dquery.reshape(query_b.shape), dkey, dvalue)


def on_device(
    tokens,
    seg_starts,
    gain_attn,
    gain_mlp,
    query_scale,
    w_query,
    w_key,
    w_value,
    w_out,
    w_up,
    w_down,
    cotangent,
):
    gathered = (
        lax.all_gather(w_query, "fsdp", axis=0, tiled=True),
        lax.all_gather(w_key, "fsdp", axis=0, tiled=True),
        lax.all_gather(w_value, "fsdp", axis=0, tiled=True),
        lax.all_gather(w_out, "fsdp", axis=1, tiled=True),
        lax.all_gather(w_up, "fsdp", axis=0, tiled=True),
        lax.all_gather(w_down, "fsdp", axis=1, tiled=True),
    )
    full_query, full_key, full_value, full_out, full_up, full_down = gathered
    local_rows = tokens.shape[0]
    row_length = local_rows * lax.axis_size("tp")
    block_rows = min(512, row_length)
    local_heads = full_query.shape[1] // HD
    positions, series = segment_ids(seg_starts[0], row_length)
    resid = tokens.astype(jnp.float32)
    scale_one = inverse_rms(resid)
    normed_one = (resid * scale_one * gain_attn).astype(jnp.bfloat16)
    gathered_one = lax.all_gather(normed_one, "tp", axis=0, tiled=True)
    query = jnp.dot(gathered_one, full_query, preferred_element_type=jnp.float32).reshape(
        row_length, local_heads, HD
    )
    scaling = softplus_unit / math.sqrt(HD) * jax.nn.softplus(query_scale)
    query_b = (query * scaling).astype(jnp.bfloat16)
    key_b = (
        jnp.dot(gathered_one, full_key, preferred_element_type=jnp.float32)
        .astype(jnp.bfloat16)
        .reshape(row_length, local_heads, HD)
    )
    value_b = (
        jnp.dot(gathered_one, full_value, preferred_element_type=jnp.float32)
        .astype(jnp.bfloat16)
        .reshape(row_length, local_heads, HD)
    )
    mixed, logsum = attend_forward(query_b, key_b, value_b, positions, series, block_rows)
    mixed_b = mixed.astype(jnp.bfloat16)
    attn_part = jnp.dot(mixed_b, full_out, preferred_element_type=jnp.float32)
    middle = resid + lax.psum_scatter(attn_part, "tp", scatter_dimension=0, tiled=True)
    scale_two = inverse_rms(middle)
    normed_two = (middle * scale_two * gain_mlp).astype(jnp.bfloat16)
    wide_up, wide_down = (full_up, full_down)
    mlp_input = lax.all_gather(normed_two, "tp", axis=0, tiled=True)
    upward = jnp.dot(mlp_input, wide_up, preferred_element_type=jnp.float32)
    activated, gelu_back = jax.vjp(jax.nn.gelu, upward)
    hidden_b = activated.astype(jnp.bfloat16)
    mlp_part = jnp.dot(hidden_b, wide_down, preferred_element_type=jnp.float32)
    mlp_sum = lax.psum_scatter(
        mlp_part.astype(jnp.bfloat16), "tp", scatter_dimension=0, tiled=True
    ).astype(jnp.float32)
    result = (middle + mlp_sum).astype(jnp.bfloat16)
    dlower = lax.all_gather(cotangent, "tp", axis=0, tiled=True)
    grad_down_here = jnp.einsum("rf,rd->fd", hidden_b, dlower, preferred_element_type=jnp.float32)
    dhidden = jnp.einsum("rd,fd->rf", dlower, wide_down, preferred_element_type=jnp.float32)
    dupward = gelu_back(dhidden)[0].astype(jnp.bfloat16)
    grad_up_here = jnp.einsum("rd,rf->df", mlp_input, dupward, preferred_element_type=jnp.float32)
    dnorm_part = jnp.einsum("rf,df->rd", dupward, wide_up, preferred_element_type=jnp.float32)
    dnormed_two = lax.psum_scatter(dnorm_part, "tp", scatter_dimension=0, tiled=True)
    grad_up_part, grad_down_part = (grad_up_here, grad_down_here)
    dresid_two, dgain_two = norm_backward(middle, scale_two, gain_mlp, dnormed_two)
    dmiddle = cotangent.astype(jnp.float32) + dresid_two
    dattn = lax.all_gather(dmiddle.astype(jnp.bfloat16), "tp", axis=0, tiled=True)
    grad_out_part = jnp.einsum("rh,rd->hd", mixed_b, dattn, preferred_element_type=jnp.float32)
    dmixed = jnp.einsum("rd,hd->rh", dattn, full_out, preferred_element_type=jnp.float32).astype(
        jnp.bfloat16
    )
    dquery_scaled, dkey, dvalue = attend_backward(
        query_b, key_b, value_b, dmixed, logsum, positions, series, block_rows
    )
    dscaling = jnp.sum(dquery_scaled * query, axis=(0, 1))
    dquery = (dquery_scaled * scaling).astype(jnp.bfloat16).reshape(row_length, local_heads * HD)
    dkey_b = dkey.astype(jnp.bfloat16).reshape(row_length, local_heads * HD)
    dvalue_b = dvalue.astype(jnp.bfloat16).reshape(row_length, local_heads * HD)
    grad_query_part = jnp.einsum(
        "rd,rh->dh", gathered_one, dquery, preferred_element_type=jnp.float32
    )
    grad_key_part = jnp.einsum(
        "rd,rh->dh", gathered_one, dkey_b, preferred_element_type=jnp.float32
    )
    grad_value_part = jnp.einsum(
        "rd,rh->dh", gathered_one, dvalue_b, preferred_element_type=jnp.float32
    )
    dnorm_one_part = jnp.einsum("rh,dh->rd", dquery, full_query, preferred_element_type=jnp.float32)
    dnorm_one_part = dnorm_one_part + jnp.einsum(
        "rh,dh->rd", dkey_b, full_key, preferred_element_type=jnp.float32
    )
    dnorm_one_part = dnorm_one_part + jnp.einsum(
        "rh,dh->rd", dvalue_b, full_value, preferred_element_type=jnp.float32
    )
    dnormed_one = lax.psum_scatter(dnorm_one_part, "tp", scatter_dimension=0, tiled=True)
    dresid_one, dgain_one = norm_backward(resid, scale_one, gain_attn, dnormed_one)
    grad_tokens = dmiddle + dresid_one
    summed = (
        lax.psum_scatter(grad_query_part, "fsdp", scatter_dimension=0, tiled=True),
        lax.psum_scatter(grad_key_part, "fsdp", scatter_dimension=0, tiled=True),
        lax.psum_scatter(grad_value_part, "fsdp", scatter_dimension=0, tiled=True),
        lax.psum_scatter(grad_out_part, "fsdp", scatter_dimension=1, tiled=True),
        lax.psum_scatter(grad_up_part, "fsdp", scatter_dimension=0, tiled=True),
        lax.psum_scatter(grad_down_part, "fsdp", scatter_dimension=1, tiled=True),
    )
    dscale_param = dscaling * (softplus_unit / math.sqrt(HD)) * jax.nn.sigmoid(query_scale)
    grad_gain_attn, grad_gain_mlp, grad_query_scale = lax.psum(
        (dgain_one, dgain_two, dscale_param), ("fsdp", "tp")
    )
    return (
        result,
        grad_tokens,
        grad_gain_attn,
        grad_gain_mlp,
        grad_query_scale,
        summed[0],
        summed[1],
        summed[2],
        summed[3],
        summed[4],
        summed[5],
    )


BF16, F32 = jnp.bfloat16, jnp.float32
RING = (0, 2, 4, 6, 7, 5, 3, 1)
CORES = tuple((i, i ^ 1) for i in range(16))
AROUND = tuple((2 * RING[i], 2 * RING[(i + 1) % 8]) for i in range(8)) + tuple(
    (2 * RING[i] + 1, 2 * RING[(i + 7) % 8] + 1) for i in range(8)
)
VMEM = pl.BlockSpec(memory_space=pltpu.VMEM)
HELD = pl.BlockSpec(memory_space=pltpu.VMEM)
LIMIT = 30 * 2**20
UNROLL = (4, 8)
SMEM = pl.BlockSpec(memory_space=pltpu.SMEM)
ANY = pl.BlockSpec(memory_space=pl.ANY)
LEAVE = (9, 6, 7, 4, 5, 2, 3, 1)
STAY = (8, 14, 15, 12, 13, 10, 11, 0)
STEPS = (1, 2, 2, 2, 1)
FAR_STEPS = (1, 2, 2, 3)


def sibling(value):
    return lax.ppermute(value, "fsdp", CORES)


def around(value):
    return lax.ppermute(value, "fsdp", AROUND)


def across(value):
    return lax.ppermute(value, "tp", ((0, 1), (1, 0)))


def arrival_order(rows):
    index = lax.axis_index("fsdp")
    chip, core = index // 2, lax.rem(index, 2)
    place = jnp.where(lax.rem(chip, 2) == 0, chip // 2, 7 - chip // 2)
    sign = 1 - 2 * core

    def shard(step, which):
        at = lax.rem(place + step + 16, 8)
        return 2 * jnp.where(at < 4, 2 * at, 15 - 2 * at) + which

    order = [shard(0, core), shard(0, 1 - core)]
    for step in (1, 2, 3):
        order += [shard(-step * sign, core), shard(-step * sign, 1 - core)]
    order += [shard(4, core), shard(4, 1 - core)]
    for step in (1, 2, 3):
        order += [shard(step * sign, 1 - core), shard(step * sign, core)]
    return jnp.stack([rows * o for o in order] + [lax.axis_index("tp")]).astype(jnp.int32)


def after(value, *others):
    return lax.optimization_barrier((value, *others))[0]


def pack_kernel(query, key, value, out, up, down, early, late):
    cols = query.shape[1]
    for n, ref in enumerate((query, key, value)):
        early[:, n * cols : (n + 1) * cols] = ref[...]
    late[:, :cols] = out[...]
    late[:, cols : 2 * cols] = up[...]
    late[:, 2 * cols :] = down[...]


def all_after(values, *others):
    return lax.optimization_barrier((*values, *others))[: len(values)]


def ring_gather(early, late, tokens, prepare):
    rows = early.shape[0]
    first = [early, sibling(early)]
    here = [late, sibling(after(late, first[1]))]
    other_tokens = across(tokens)
    there = [across(after(late, other_tokens))]
    first.append(around(jnp.concatenate(first)))
    here.append(around(jnp.concatenate(here)))
    first.append(around(after(first[2], other_tokens)))
    here.append(around(here[2]))
    there.append(across(here[2]))
    first.append(around(after(first[3], there[0])))
    here.append(around(here[3]))
    there.append(across(here[3]))
    prepared = prepare(other_tokens)
    first.append(around(after(first[4][:rows], prepared, there[1])))
    here.append(around(here[4][:rows]))
    there.append(across(here[4]))
    there.append(across(here[5]))
    first += [sibling(after(first[5], here[5]))] + [sibling(first[n]) for n in (2, 3, 4)]
    return (first, here, there, prepared, other_tokens)


def swap_late(here, there, *wait):
    there = [there[0], sibling(there[0])] + there[1:]
    return [
        got + [sibling(after(got[n], *wait)) for n in (5, 2, 3, 4)] for got in (here, there)
    ]


def total(*terms):
    out = terms[0].astype(F32)
    for term in terms[1:]:
        out = out + term.astype(F32)
    return out


class Scatter:
    def __init__(self, parts, far=None, note=None):
        self.came_from = [sibling(part) for part in parts[:5]]
        self.stay = parts[5:]
        self.far = far
        self.rows, self.cols = self.stay[0].shape
        self.came = None
        self.note = note
        self.notes = []

    def step(self, number, *wait):
        terms = [self.stay[number], self.came_from[number]]
        rows = STEPS[number] * self.rows
        note = self.note is not None
        if self.far is not None:
            terms.append(self.far[number])
        if self.came is not None:
            terms.append(self.came)
        elif note:
            terms.append(self.note)
        if number == 0 and note:
            body = first_kernel
        else:
            body = functools.partial(add_kernel, number, note)
        out = struct(rows + (16 if note else 0), self.cols)
        sent = call(body, terms, [HELD] * len(terms), [(out, HELD)], [], 10**6)[0]
        self.sent = sent
        came = around(after(sent, *wait) if wait else sent)
        if note:
            self.notes.append(came[rows:])
        self.came = came
        return came

    def finish(self):
        rows = self.rows
        came = self.came
        terms = [self.stay[4], self.came_from[4], came[rows : 2 * rows], sibling(came[:rows])]
        if self.far is not None:
            terms.append(self.far[4])
        return total(*terms)


def dot(a, b, dims):
    return lax.dot_general(a, b, (dims, ((), ())), preferred_element_type=F32)


NN, NT = ((1,), (0,)), ((1,), (1,))


def put_shards(order, pieces, target, sems):
    rows = pieces[0].shape[0]
    copies = []
    for n, piece in enumerate(pieces[:2]):
        to = pl.ds(pl.multiple_of(order[n], 16), rows)
        copies.append(load(piece, target.at[to, :], sems.at[n]))
    n = 2
    for piece in pieces[2:]:
        for part in range(piece.shape[0] // rows):
            to = pl.ds(pl.multiple_of(order[n], 16), rows)
            target[to, :] = piece[part * rows : (part + 1) * rows, :]
            n += 1
    wait_all(copies)


def load(source, target, sem):
    copy = pltpu.make_async_copy(source, target, sem)
    copy.start()
    return copy


def wait_all(copies):
    for copy in copies:
        copy.wait()


def allowed_bias(starts, bias):
    length = bias.shape[0]
    key_pos = lax.broadcasted_iota(jnp.int32, (length, 1), 0)
    query_pos = lax.broadcasted_iota(jnp.int32, (1, length), 1)
    key_series = jnp.zeros((length, 1), jnp.int32)
    query_series = jnp.zeros((1, length), jnp.int32)
    for n in range(starts.shape[1]):
        key_series += (starts[0, n] <= key_pos).astype(jnp.int32)
        query_series += (starts[0, n] <= query_pos).astype(jnp.int32)
    allowed = (key_pos <= query_pos) & (key_series == query_series)
    bias[...] = jnp.where(allowed, 0.0, -1e30).astype(F32)


def attend_kernel(heads, order, starts, scaling, normed, *rest):
    pieces, rest = rest[:10], rest[10:]
    keep, send, logsum, proj_out, weights_out, proj_t, weights, bias, scores, mixed, sems = rest
    cols = heads * HD
    length = normed.shape[0]
    allowed_bias(starts, bias)
    put_shards(order, pieces, weights, sems)
    stores = [load(weights, weights_out, sems.at[2])]
    for n in range(3):
        part = dot(normed[...], weights[:, n * cols : (n + 1) * cols], NN)
        if n == 0:
            part = part * scaling[...]
        proj_t[n * cols : (n + 1) * cols, :] = part.astype(BF16).T
    stores.append(load(proj_t, proj_out, sems.at[3]))
    blocks = ((0, length // 2), (length // 2, length))

    def rows(n, h):
        return pl.ds(pl.multiple_of(n * cols + h * HD, 16), HD)

    def one_head(h, slot):
        query = proj_t[rows(0, h), :]
        key = proj_t[rows(1, h), :].T
        value = proj_t[rows(2, h), :]
        for start, stop in blocks:
            scores[slot, :stop, start:stop] = dot(key[:stop], query[:, start:stop], NN)
        for start, stop in blocks:
            part = scores[slot, :stop, start:stop] + bias[:stop, start:stop]
            row_max = jnp.max(part, axis=0, keepdims=True)
            exponent = jnp.exp(part - row_max)
            total = jnp.sum(exponent, axis=0, keepdims=True)
            soft_b = (exponent * (1.0 / total)).astype(BF16)
            mixed[rows(0, h), start:stop] = dot(value[:, :stop], soft_b, NN).astype(BF16)
            logsum[h, :, start:stop] = row_max + jnp.log(total)

    @pl.loop(0, heads // UNROLL[0])
    def _(block):
        for n in range(UNROLL[0]):
            one_head(block * UNROLL[0] + n, n)

    half = order[16]
    low, high = mixed[:, : length // 2], mixed[:, length // 2 :]
    keep[...] = jnp.where(half == 0, low, high)
    send[...] = jnp.where(half == 0, high, low)
    wait_all(stores)


def assemble_kernel(order, *rest):
    here, there, (weights, sems) = rest[:10], rest[10:20], rest[20:]
    put_shards(order, here, weights.at[0], sems)
    put_shards(order, there, weights.at[1], sems)


def middle_kernel(
    tokens, cot, gain, keep, came, weights,
    dkeep, dsend, hidden_o, dup_o, normed_o, dattn_o, mixed_o, middle_o, dgain_o, dmiddle_out,
    dhidden, dmiddle_o, sem,
):
    cols = keep.shape[0]
    out, up, down = (slice(n * cols, (n + 1) * cols) for n in range(3))

    def half(n):
        return pl.ds(pl.multiple_of(n * cols, 128), cols)

    mixed_o[:, :cols] = keep[...].T
    mixed_o[:, cols:] = came[...].T
    middle_o[...] = tokens[...].astype(F32)

    @pl.loop(0, 2)
    def _(n):
        middle_o[...] += dot(mixed_o[:, half(n)], weights[n, :, out], NT)
        dhidden[:, half(n)] = dot(cot[...], weights[n, :, down], NN)

    middle = middle_o[...]
    scale = lax.rsqrt(jnp.mean(middle * middle, axis=-1, keepdims=True) + epsilon)
    normed_o[...] = (middle * scale * gain[...]).astype(BF16)

    @pl.loop(0, 2)
    def _(n):
        u = dot(normed_o[...], weights[n, :, up], NN)
        root = math.sqrt(2.0 / math.pi)
        square = u * u
        tanh = jnp.tanh(root * u * (1.0 + 0.044715 * square))
        gate = 0.5 * (1.0 + tanh)
        hidden_o[:, half(n)] = (u * gate).astype(BF16)
        slope = gate + 0.5 * u * (1.0 - tanh * tanh) * (root * (1.0 + 3 * 0.044715 * square))
        dup_o[:, half(n)] = (dhidden[:, half(n)] * slope).astype(BF16)

    dmiddle_o[...] = jnp.zeros_like(dmiddle_o)

    @pl.loop(0, 2)
    def _(n):
        dmiddle_o[...] += dot(dup_o[:, half(n)], weights[n, :, up], NT)

    dnormed = dmiddle_o[...]
    middle = middle_o[...]
    dgain_o[...] = jnp.sum(dnormed * middle * scale, axis=0, keepdims=True)
    weighted = dnormed * gain[...]
    mean = jnp.mean(weighted * middle, axis=-1, keepdims=True)
    dmiddle = cot[...].astype(F32) + scale * weighted - middle * (scale * scale * scale * mean)
    dmiddle_o[...] = dmiddle
    store = load(dmiddle_o, dmiddle_out, sem)
    dattn_o[...] = dmiddle.astype(BF16)
    for n, ref in enumerate((dkeep, dsend)):
        ref[...] = dot(dattn_o[...], weights[n, :, out], NN).astype(BF16).T
    store.wait()


def by_arrival(order, source_t, target, rows):
    for n, which in enumerate(LEAVE + STAY):
        target[n * rows : (n + 1) * rows, :] = source_t[
            pl.ds(pl.multiple_of(order[which], 16), rows), :
        ]


def split_rows(steps, rows, at=0):
    out = []
    for count in steps:
        out.append(slice(at, at + count * rows))
        at += count * rows
    return out


def late_grads_kernel(order, hidden, dup, normed, dattn, mixed, middle, weights, cot, *rest):
    outs, (grads, result, left_t, left, sems) = rest[:19], rest[19:]
    cols = dup.shape[1] // 2
    rows = dup.shape[1] // 16
    pairs = ((dattn, mixed), (normed, dup), (cot, hidden))
    for n, (a, _) in enumerate(pairs):
        left_t[n, :, :] = a[...].T
        by_arrival(order, left_t.at[n], left.at[n], rows)
    stores = []
    for leaves in range(2):
        top = leaves * 8 * rows
        part = slice(top, top + 8 * rows)
        for side, steps, start in ((1, FAR_STEPS, 10), (0, STEPS, 0)):
            for n, (_, b) in enumerate(pairs):
                grads[side, part, n * cols : (n + 1) * cols] = dot(
                    left[n, part, :], b[:, side * cols : (side + 1) * cols], NN
                ).astype(BF16)
            start += leaves * len(steps)
            for k, at in enumerate(split_rows(steps, rows, top)):
                stores.append(load(grads.at[side, at, :], outs[start + k], sems.at[start + k]))
    total = middle[...]
    for side in range(2):
        at = slice(side * cols, (side + 1) * cols)
        total = total + dot(hidden[:, at], weights[side, :, 2 * cols :], NT)
    result[...] = total.astype(BF16)
    stores.append(load(result, outs[18], sems.at[18]))
    wait_all(stores)


def attend_back_kernel(
    heads, order, starts, scaling_col, keep, came, logsum, proj_in, weights_in, tokens_in, other_in,
    dscaling, dgain, dproj_out, keep_out, send_out,
    weights, proj_t, bias, dmixed, dproj_t, scores, dsofts, dproj, kept, sent, tokens, sems,
):
    fetch = load(proj_in, proj_t, sems.at[0])
    fetch_late = [
        load(weights_in, weights, sems.at[1]),
        load(tokens_in, tokens.at[0], sems.at[2]),
        load(other_in, tokens.at[1], sems.at[3]),
    ]
    cols = heads * HD
    length = proj_t.shape[1]
    rows = length // 2
    allowed_bias(starts, bias)
    half = order[16]
    dmixed[:, :rows] = jnp.where(half == 0, keep[...], came[...])
    dmixed[:, rows:] = jnp.where(half == 0, came[...], keep[...])
    fetch.wait()
    dscaling[...] = jnp.zeros_like(dscaling)

    def place(n, h):
        return pl.ds(pl.multiple_of(n * cols + h * HD, 16), HD)

    def one_head(h, slot):
        query = proj_t[place(0, h), :]
        key_t = proj_t[place(1, h), :]
        key = key_t.T
        value = proj_t[place(2, h), :].T
        grad = dmixed[place(0, h), :]
        for start, stop in ((0, rows), (rows, length)):
            scores[slot, :stop, start:stop] = dot(key[:stop], query[:, start:stop], NN)
            dsofts[slot, :stop, start:stop] = dot(value[:stop], grad[:, start:stop], NN)
        parts = []
        for start, stop in ((rows, length), (0, rows)):
            soft = scores[slot, :stop, start:stop] + bias[:stop, start:stop]
            soft = jnp.exp(soft - logsum[h, :, start:stop])
            dsoft = dsofts[slot, :stop, start:stop]
            inner = jnp.sum(soft * dsoft, axis=0, keepdims=True)
            dscores = (soft * (dsoft - inner)).astype(BF16)
            dquery = dot(key_t[:, :stop], dscores, NN)
            dscaling[...] += jnp.sum(
                dquery * query[:, start:stop].astype(F32), axis=1, keepdims=True
            )
            dproj_t[place(0, h), start:stop] = (dquery * scaling_col[...]).astype(BF16)
            parts.append(
                (dot(dscores, query[:, start:stop], NT), dot(soft.astype(BF16), grad[:, start:stop], NT))
            )
        for n in range(2):
            both = jnp.concatenate([parts[0][n][:rows] + parts[1][n], parts[0][n][rows:]], axis=0)
            dproj_t[place(n + 1, h), :] = both.astype(BF16).T

    @pl.loop(0, heads // UNROLL[1])
    def _(block):
        for n in range(UNROLL[1]):
            one_head(block * UNROLL[1] + n, n % 2)

    dproj[...] = dproj_t[...].T
    stores = [load(dproj, dproj_out, sems.at[4])]
    wait_all(fetch_late)
    parts = []
    total = jnp.zeros(dgain.shape, F32)
    for n in range(2):
        part = dot(dproj[n * rows : (n + 1) * rows, :], weights[...], NT)
        resid = jnp.where(half == n, tokens[0], tokens[1]).astype(F32)
        scale = lax.rsqrt(jnp.mean(resid * resid, axis=-1, keepdims=True) + epsilon)
        total = total + jnp.sum(part * resid * scale, axis=0, keepdims=True)
        parts.append(part)
    dgain[...] = total
    sent[...] = jnp.where(half == 0, parts[1], parts[0]).astype(BF16)
    stores.append(load(sent, send_out, sems.at[5]))
    kept[...] = jnp.where(half == 0, parts[0], parts[1])
    stores.append(load(kept, keep_out, sems.at[6]))
    wait_all(stores)


def early_grads_kernel(order, normed, dproj_in, *rest):
    outs, (dproj, grads, left_t, left, sems) = rest[:10], rest[10:]
    fetch = load(dproj_in, dproj, sems.at[10])
    rows = normed.shape[1] // 16
    left_t[...] = normed[...].T
    by_arrival(order, left_t, left, rows)
    fetch.wait()
    stores = []
    for leaves in range(2):
        top = leaves * 8 * rows
        part = slice(top, top + 8 * rows)
        grads[part, :] = dot(left[part, :], dproj[...], NN).astype(BF16)
        for k, at in enumerate(split_rows(STEPS, rows, top)):
            n = 5 * leaves + k
            stores.append(load(grads.at[at, :], outs[n], sems.at[n]))
    wait_all(stores)


def first_kernel(stay, came, note, out):
    rows = stay.shape[0]
    out[:rows, :] = (stay[...].astype(F32) + came[...].astype(F32)).astype(BF16)
    out[rows:, :] = note[...]


def add_kernel(number, note, *rest):
    *terms, out = rest
    rows = terms[0].shape[0]
    late = terms.pop() if number > 0 else None
    part = terms[0][...].astype(F32)
    for term in terms[1:]:
        part = part + term[...].astype(F32)
    if number == 1:
        half = rows // 2
        out[:half, :] = part[:half].astype(BF16)
        out[half:rows, :] = (part[half:] + late[:half, :].astype(F32)).astype(BF16)
    else:
        if late is not None:
            part = part + late[:rows, :].astype(F32)
        out[:rows, :] = part.astype(BF16)
    if note:
        out[rows:, :] = late[late.shape[0] - 16 :, :]


def pair_kernel(one, other, out):
    out[...] = (one[...].astype(F32) + other[...].astype(F32)).astype(BF16)


def struct(*shape, kind=BF16):
    return jax.ShapeDtypeStruct(shape, kind)


def call(body, inputs, spaces, outputs, scratch, flops):
    place = {id(HELD): pltpu.VMEM, id(ANY): pltpu.HBM, id(VMEM): pltpu.HBM}
    inputs = [
        pltpu.with_memory_space_constraint(value, place[id(space)]) if id(space) in place else value
        for value, space in zip(inputs, spaces)
    ]
    return pl.pallas_call(
        body,
        out_shape=[place[id(space)](out.shape, out.dtype) for out, space in outputs],
        in_specs=[VMEM if space is HELD else space for space in spaces],
        out_specs=[VMEM if space is HELD else space for _, space in outputs],
        scratch_shapes=scratch,
        compiler_params=pltpu.CompilerParams(vmem_limit_bytes=LIMIT),
        cost_estimate=pl.CostEstimate(flops=flops * 4, bytes_accessed=2**22, transcendentals=0),
    )(*inputs)


def in_order(half, own, other, axis=0):
    return jnp.where(
        half == 0,
        jnp.concatenate([own, other], axis=axis),
        jnp.concatenate([other, own], axis=axis),
    )


def on_slice(
    tokens,
    seg_starts,
    gain_attn,
    gain_mlp,
    query_scale,
    w_query,
    w_key,
    w_value,
    w_out,
    w_up,
    w_down,
    cotangent,
):
    half = lax.axis_index("tp")
    rows, width = tokens.shape
    shard, cols = w_query.shape
    length = 2 * rows
    heads = cols // HD
    dma = pltpu.SemaphoreType.DMA
    order = arrival_order(shard)
    early, late = call(
        pack_kernel,
        [w_query, w_key, w_value, w_out.T, w_up, w_down.T],
        [VMEM] * 6,
        [(struct(shard, 3 * cols), VMEM)] * 2,
        [],
        10**6,
    )

    def prepare(other_tokens):
        row_tokens = in_order(half, tokens, other_tokens).astype(F32)
        return (row_tokens * inverse_rms(row_tokens) * gain_attn).astype(BF16)

    first, here, there, normed, other_tokens = ring_gather(early, late, tokens, prepare)
    scaling = softplus_unit / math.sqrt(HD) * jax.nn.softplus(query_scale)
    keep, send, logsum, proj_t, w_in = call(
        functools.partial(attend_kernel, heads),
        [after(order, there[2]), seg_starts, jnp.tile(scaling, heads)[None, :], normed]
        + first,
        [SMEM] * 2 + [HELD] * 2 + [ANY] * 2 + [HELD] * 8,
        [
            (struct(cols, rows), HELD),
            (struct(cols, rows), HELD),
            (struct(heads, 1, length, kind=F32), HELD),
            (struct(3 * cols, length), ANY),
            (struct(width, 3 * cols), ANY),
        ],
        [
            pltpu.VMEM((3 * cols, length), BF16),
            pltpu.VMEM((width, 3 * cols), BF16),
            pltpu.VMEM((length, length), F32),
            pltpu.VMEM((UNROLL[0], length, length), F32),
            pltpu.VMEM((cols, length), BF16),
            dma((4,)),
        ],
        8 * 10**9,
    )
    came = across(send)
    here, there = swap_late(here, there, logsum)
    w_late = call(
        assemble_kernel,
        [after(order, came), *here, *there],
        [SMEM] + ([ANY] * 2 + [HELD] * 8) * 2,
        [(struct(2, width, 3 * cols), HELD)],
        [dma((2,))],
        10**6,
    )[0]
    act = struct(rows, width)
    dkeep, dsend, *saved, dgain_two, dmiddle = call(
        middle_kernel,
        [tokens, cotangent, gain_mlp[None, :], keep, came, w_late],
        [HELD] * 6,
        [(struct(cols, rows), HELD)] * 2
        + [(act, HELD)] * 5
        + [
            (struct(rows, width, kind=F32), HELD),
            (struct(1, width, kind=F32), HELD),
            (struct(rows, width, kind=F32), ANY),
        ],
        [pltpu.VMEM((rows, width), F32), pltpu.VMEM((rows, width), F32), dma],
        8 * 10**9,
    )
    dcame = across(dsend)
    *parts, result = call(
        late_grads_kernel,
        [order, *saved, w_late, cotangent],
        [SMEM] + [HELD] * 8,
        [(struct(n * shard, 3 * cols), ANY) for n in STEPS * 2 + FAR_STEPS * 2] + [(act, ANY)],
        [
            pltpu.VMEM((2, width, 3 * cols), BF16),
            pltpu.VMEM((rows, width), BF16),
            pltpu.VMEM((3, width, rows), BF16),
            pltpu.VMEM((3, width, rows), BF16),
            dma((19,)),
        ],
        6 * 10**9,
    )
    *parts, result = all_after((*parts, result), dcame)
    far, far_sent = [], []
    for n, steps in enumerate(FAR_STEPS):
        pair = [parts[14 + n], sibling(parts[10 + n])]
        sent = call(pair_kernel, pair, [HELD] * 2, [(struct(steps * shard, 3 * cols), HELD)], [], 10**6)
        far_sent += sent
        far.append(across(sent[0]))
    far_last = far.pop()
    far += [far_last[: 2 * shard], far_last[2 * shard :]]
    late_sum = Scatter(parts[:10], far)
    late_one = late_sum.step(0)
    dscaling, dgain_one, dproj, dnormed, dnormed_send = call(
        functools.partial(attend_back_kernel, heads),
        [
            after(order, late_sum.came_from[0]),
            seg_starts,
            scaling[:, None],
            dkeep,
            dcame,
            logsum,
            proj_t,
            w_in,
            tokens,
            other_tokens,
        ],
        [SMEM] * 2 + [HELD] * 4 + [ANY] * 4,
        [
            (struct(HD, 1, kind=F32), HELD),
            (struct(1, width, kind=F32), HELD),
            (struct(length, 3 * cols), ANY),
            (struct(rows, width, kind=F32), ANY),
            (act, ANY),
        ],
        [
            pltpu.VMEM((width, 3 * cols), BF16),
            pltpu.VMEM((3 * cols, length), BF16),
            pltpu.VMEM((length, length), F32),
            pltpu.VMEM((cols, length), BF16),
            pltpu.VMEM((3 * cols, length), BF16),
            pltpu.VMEM((2, length, length), F32),
            pltpu.VMEM((2, length, length), F32),
            pltpu.VMEM((length, 3 * cols), BF16),
            pltpu.VMEM((rows, width), F32),
            pltpu.VMEM((rows, width), BF16),
            pltpu.VMEM((2, rows, width), BF16),
            dma((7,)),
        ],
        12 * 10**9,
    )
    dscaling, dgain_one, dproj, dnormed, dnormed_send = all_after(
        (dscaling, dgain_one, dproj, dnormed, dnormed_send), *far[:2]
    )
    dscale_param = (
        dscaling[:, 0] / scaling * (softplus_unit / math.sqrt(HD)) * jax.nn.sigmoid(query_scale)
    )
    note = jnp.concatenate(
        [
            jnp.concatenate([dgain_one, jnp.pad(dscale_param[None, :], ((0, 0), (0, cols - HD)))], axis=1),
            jnp.pad(dgain_two, ((0, 0), (0, cols))),
        ]
    )
    parts = call(
        early_grads_kernel,
        [after(order, far_sent[2]), normed, dproj],
        [SMEM, HELD, ANY],
        [(struct(n * shard, 3 * cols), ANY) for n in STEPS + STEPS],
        [
            pltpu.VMEM((length, 3 * cols), BF16),
            pltpu.VMEM((width, 3 * cols), BF16),
            pltpu.VMEM((width, length), BF16),
            pltpu.VMEM((width, length), BF16),
            dma((11,)),
        ],
        5 * 10**9,
    )
    note = note + sibling(after(note, parts[1]))
    high = lax.reduce_precision(note, 8, 7)
    coded = jnp.concatenate([high, note - high, jnp.zeros((12, 3 * cols), F32)]).astype(BF16)
    parts = all_after(parts, late_one)
    late_two = late_sum.step(1)
    early_sum = Scatter(parts, note=coded)
    early_sum.step(0)
    late_three = late_sum.step(2)
    early_sum.came = after(early_sum.came, late_two)
    early_sum.step(1)
    late_four = late_sum.step(3)
    early_three = early_sum.step(2)
    dnormed = dnormed + after(across(dnormed_send), early_three).astype(F32)
    resid = tokens.astype(F32)
    dresid_one, _ = norm_backward(resid, inverse_rms(resid), gain_attn, dnormed)
    early_sum.came = after(early_sum.came, late_three, far[3])
    early_sum.step(3)
    late_sum.came = after(late_sum.came, early_sum.sent)
    dlate = late_sum.finish()
    din = early_sum.finish()
    mine = early_sum.notes
    core = lax.rem(lax.axis_index("fsdp"), 2)
    heard = total(*mine[:3]) + jnp.where(core == 0, 1.0, 0.0) * mine[3].astype(F32)
    heard = heard[:2] + heard[2:4]
    heard = heard + sibling(heard)
    small = note + heard
    small = small + across(small)
    return (
        result,
        dmiddle + dresid_one,
        small[0, :width],
        small[1, :width],
        small[0, width : width + HD],
        din[:, :cols],
        din[:, cols : 2 * cols],
        din[:, 2 * cols :],
        dlate[:, :cols].T,
        dlate[:, cols : 2 * cols],
        dlate[:, 2 * cols :].T,
    )


def solution(mesh):
    body = on_slice if dict(mesh.shape) == {"fsdp": 16, "tp": 2} else on_device
    placed = (
        P(("fsdp", "tp"), None),
        P("fsdp", None),
        P(),
        P(),
        P(),
        P("fsdp", "tp"),
        P("fsdp", "tp"),
        P("fsdp", "tp"),
        P("tp", "fsdp"),
        P("fsdp", "tp"),
        P("tp", "fsdp"),
        P(("fsdp", "tp"), None),
    )
    return jax.shard_map(
        body,
        mesh=mesh,
        in_specs=placed,
        out_specs=(
            P(("fsdp", "tp"), None),
            P(("fsdp", "tp"), None),
            P(),
            P(),
            P(),
            P("fsdp", "tp"),
            P("fsdp", "tp"),
            P("fsdp", "tp"),
            P("tp", "fsdp"),
            P("fsdp", "tp"),
            P("tp", "fsdp"),
        ),
        check_vma=False,
    )
```

```python
import functools
import math

import jax
import jax.numpy as jnp
from jax import lax
from jax.experimental import pallas as pl
from jax.experimental.pallas import tpu as pltpu
from jax.sharding import PartitionSpec as P

HD = 80


epsilon = 1e-06
softplus_unit = 1.442695041


def inverse_rms(values):
    return lax.rsqrt(jnp.mean(values * values, axis=-1, keepdims=True) + epsilon)


def norm_backward(resid, inv_scale, gain, dnormed):
    weighted = dnormed * gain
    cubed = inv_scale * inv_scale * inv_scale
    dresid = inv_scale * weighted - resid * cubed * jnp.mean(
        weighted * resid, axis=-1, keepdims=True
    )
    dgain = jnp.sum(dnormed * resid * inv_scale, axis=0)
    return (dresid, dgain)


def segment_ids(starts, length):
    positions = jnp.arange(length, dtype=jnp.int32)
    inside = (starts[None, :] <= positions[:, None]).astype(jnp.int32)
    return (positions, jnp.sum(inside, axis=1) - 1)


def block_scores(query_blk, block_pos, block_series, key_b, positions, series):
    scores = jnp.einsum("qhd,khd->hqk", query_blk, key_b, preferred_element_type=jnp.float32)
    allowed = (positions[None, :] <= block_pos[:, None]) & (
        series[None, :] == block_series[:, None]
    )
    return jnp.where(allowed[None], scores, -1e30)


def attend_forward(query_b, key_b, value_b, positions, series, block_rows):
    num_blocks = query_b.shape[0] // block_rows
    local_heads = query_b.shape[1]

    def one_block(inputs):
        query_blk, block_pos, block_series = inputs
        scores = block_scores(query_blk, block_pos, block_series, key_b, positions, series)
        row_max = jnp.max(scores, axis=-1, keepdims=True)
        exponent = jnp.exp(scores - row_max)
        total = jnp.sum(exponent, axis=-1, keepdims=True)
        soft_b = (exponent / total).astype(jnp.bfloat16)
        mixed = jnp.einsum("hqk,khd->qhd", soft_b, value_b, preferred_element_type=jnp.float32)
        return (mixed, row_max + jnp.log(total))

    mixed, logsum = lax.map(
        one_block,
        (
            query_b.reshape(num_blocks, block_rows, local_heads, HD),
            positions.reshape(num_blocks, block_rows),
            series.reshape(num_blocks, block_rows),
        ),
    )
    return (mixed.reshape(query_b.shape[0], local_heads * HD), logsum)


def attend_backward(query_b, key_b, value_b, dmixed, logsum, positions, series, block_rows):
    num_blocks = query_b.shape[0] // block_rows
    local_heads = query_b.shape[1]

    def one_block(carry, inputs):
        dkey, dvalue = carry
        query_blk, dmixed_blk, block_pos, block_series, logsum_blk = inputs
        scores = block_scores(query_blk, block_pos, block_series, key_b, positions, series)
        soft = jnp.exp(scores - logsum_blk)
        dsoft = jnp.einsum("qhd,khd->hqk", dmixed_blk, value_b, preferred_element_type=jnp.float32)
        inner = jnp.sum(soft * dsoft, axis=-1, keepdims=True)
        dscores = (soft * (dsoft - inner)).astype(jnp.bfloat16)
        dquery_blk = jnp.einsum("hqk,khd->qhd", dscores, key_b, preferred_element_type=jnp.float32)
        dkey = dkey + jnp.einsum(
            "hqk,qhd->khd", dscores, query_blk, preferred_element_type=jnp.float32
        )
        dvalue = dvalue + jnp.einsum(
            "hqk,qhd->khd",
            soft.astype(jnp.bfloat16),
            dmixed_blk,
            preferred_element_type=jnp.float32,
        )
        return ((dkey, dvalue), dquery_blk)

    zeros = jnp.zeros(key_b.shape, jnp.float32)
    inputs = (
        query_b.reshape(num_blocks, block_rows, local_heads, HD),
        dmixed.reshape(num_blocks, block_rows, local_heads, HD),
        positions.reshape(num_blocks, block_rows),
        series.reshape(num_blocks, block_rows),
        logsum,
    )
    (dkey, dvalue), dquery = lax.scan(one_block, (zeros, zeros), inputs)
    return (dquery.reshape(query_b.shape), dkey, dvalue)


def on_device(
    tokens,
    seg_starts,
    gain_attn,
    gain_mlp,
    query_scale,
    w_query,
    w_key,
    w_value,
    w_out,
    w_up,
    w_down,
    cotangent,
):
    gathered = (
        lax.all_gather(w_query, "fsdp", axis=0, tiled=True),
        lax.all_gather(w_key, "fsdp", axis=0, tiled=True),
        lax.all_gather(w_value, "fsdp", axis=0, tiled=True),
        lax.all_gather(w_out, "fsdp", axis=1, tiled=True),
        lax.all_gather(w_up, "fsdp", axis=0, tiled=True),
        lax.all_gather(w_down, "fsdp", axis=1, tiled=True),
    )
    full_query, full_key, full_value, full_out, full_up, full_down = gathered
    local_rows = tokens.shape[0]
    row_length = local_rows * lax.axis_size("tp")
    block_rows = min(512, row_length)
    local_heads = full_query.shape[1] // HD
    positions, series = segment_ids(seg_starts[0], row_length)
    resid = tokens.astype(jnp.float32)
    scale_one = inverse_rms(resid)
    normed_one = (resid * scale_one * gain_attn).astype(jnp.bfloat16)
    gathered_one = lax.all_gather(normed_one, "tp", axis=0, tiled=True)
    query = jnp.dot(gathered_one, full_query, preferred_element_type=jnp.float32).reshape(
        row_length, local_heads, HD
    )
    scaling = softplus_unit / math.sqrt(HD) * jax.nn.softplus(query_scale)
    query_b = (query * scaling).astype(jnp.bfloat16)
    key_b = (
        jnp.dot(gathered_one, full_key, preferred_element_type=jnp.float32)
        .astype(jnp.bfloat16)
        .reshape(row_length, local_heads, HD)
    )
    value_b = (
        jnp.dot(gathered_one, full_value, preferred_element_type=jnp.float32)
        .astype(jnp.bfloat16)
        .reshape(row_length, local_heads, HD)
    )
    mixed, logsum = attend_forward(query_b, key_b, value_b, positions, series, block_rows)
    mixed_b = mixed.astype(jnp.bfloat16)
    attn_part = jnp.dot(mixed_b, full_out, preferred_element_type=jnp.float32)
    middle = resid + lax.psum_scatter(attn_part, "tp", scatter_dimension=0, tiled=True)
    scale_two = inverse_rms(middle)
    normed_two = (middle * scale_two * gain_mlp).astype(jnp.bfloat16)
    wide_up, wide_down = (full_up, full_down)
    mlp_input = lax.all_gather(normed_two, "tp", axis=0, tiled=True)
    upward = jnp.dot(mlp_input, wide_up, preferred_element_type=jnp.float32)
    activated, gelu_back = jax.vjp(jax.nn.gelu, upward)
    hidden_b = activated.astype(jnp.bfloat16)
    mlp_part = jnp.dot(hidden_b, wide_down, preferred_element_type=jnp.float32)
    mlp_sum = lax.psum_scatter(
        mlp_part.astype(jnp.bfloat16), "tp", scatter_dimension=0, tiled=True
    ).astype(jnp.float32)
    result = (middle + mlp_sum).astype(jnp.bfloat16)
    dlower = lax.all_gather(cotangent, "tp", axis=0, tiled=True)
    grad_down_here = jnp.einsum("rf,rd->fd", hidden_b, dlower, preferred_element_type=jnp.float32)
    dhidden = jnp.einsum("rd,fd->rf", dlower, wide_down, preferred_element_type=jnp.float32)
    dupward = gelu_back(dhidden)[0].astype(jnp.bfloat16)
    grad_up_here = jnp.einsum("rd,rf->df", mlp_input, dupward, preferred_element_type=jnp.float32)
    dnorm_part = jnp.einsum("rf,df->rd", dupward, wide_up, preferred_element_type=jnp.float32)
    dnormed_two = lax.psum_scatter(dnorm_part, "tp", scatter_dimension=0, tiled=True)
    grad_up_part, grad_down_part = (grad_up_here, grad_down_here)
    dresid_two, dgain_two = norm_backward(middle, scale_two, gain_mlp, dnormed_two)
    dmiddle = cotangent.astype(jnp.float32) + dresid_two
    dattn = lax.all_gather(dmiddle.astype(jnp.bfloat16), "tp", axis=0, tiled=True)
    grad_out_part = jnp.einsum("rh,rd->hd", mixed_b, dattn, preferred_element_type=jnp.float32)
    dmixed = jnp.einsum("rd,hd->rh", dattn, full_out, preferred_element_type=jnp.float32).astype(
        jnp.bfloat16
    )
    dquery_scaled, dkey, dvalue = attend_backward(
        query_b, key_b, value_b, dmixed, logsum, positions, series, block_rows
    )
    dscaling = jnp.sum(dquery_scaled * query, axis=(0, 1))
    dquery = (dquery_scaled * scaling).astype(jnp.bfloat16).reshape(row_length, local_heads * HD)
    dkey_b = dkey.astype(jnp.bfloat16).reshape(row_length, local_heads * HD)
    dvalue_b = dvalue.astype(jnp.bfloat16).reshape(row_length, local_heads * HD)
    grad_query_part = jnp.einsum(
        "rd,rh->dh", gathered_one, dquery, preferred_element_type=jnp.float32
    )
    grad_key_part = jnp.einsum(
        "rd,rh->dh", gathered_one, dkey_b, preferred_element_type=jnp.float32
    )
    grad_value_part = jnp.einsum(
        "rd,rh->dh", gathered_one, dvalue_b, preferred_element_type=jnp.float32
    )
    dnorm_one_part = jnp.einsum("rh,dh->rd", dquery, full_query, preferred_element_type=jnp.float32)
    dnorm_one_part = dnorm_one_part + jnp.einsum(
        "rh,dh->rd", dkey_b, full_key, preferred_element_type=jnp.float32
    )
    dnorm_one_part = dnorm_one_part + jnp.einsum(
        "rh,dh->rd", dvalue_b, full_value, preferred_element_type=jnp.float32
    )
    dnormed_one = lax.psum_scatter(dnorm_one_part, "tp", scatter_dimension=0, tiled=True)
    dresid_one, dgain_one = norm_backward(resid, scale_one, gain_attn, dnormed_one)
    grad_tokens = dmiddle + dresid_one
    summed = (
        lax.psum_scatter(grad_query_part, "fsdp", scatter_dimension=0, tiled=True),
        lax.psum_scatter(grad_key_part, "fsdp", scatter_dimension=0, tiled=True),
        lax.psum_scatter(grad_value_part, "fsdp", scatter_dimension=0, tiled=True),
        lax.psum_scatter(grad_out_part, "fsdp", scatter_dimension=1, tiled=True),
        lax.psum_scatter(grad_up_part, "fsdp", scatter_dimension=0, tiled=True),
        lax.psum_scatter(grad_down_part, "fsdp", scatter_dimension=1, tiled=True),
    )
    dscale_param = dscaling * (softplus_unit / math.sqrt(HD)) * jax.nn.sigmoid(query_scale)
    grad_gain_attn, grad_gain_mlp, grad_query_scale = lax.psum(
        (dgain_one, dgain_two, dscale_param), ("fsdp", "tp")
    )
    return (
        result,
        grad_tokens,
        grad_gain_attn,
        grad_gain_mlp,
        grad_query_scale,
        summed[0],
        summed[1],
        summed[2],
        summed[3],
        summed[4],
        summed[5],
    )


BF16, F32 = jnp.bfloat16, jnp.float32
RING = (0, 2, 4, 6, 7, 5, 3, 1)
CORES = tuple((i, i ^ 1) for i in range(16))
AROUND = tuple((2 * RING[i], 2 * RING[(i + 1) % 8]) for i in range(8)) + tuple(
    (2 * RING[i] + 1, 2 * RING[(i + 7) % 8] + 1) for i in range(8)
)
VMEM = pl.BlockSpec(memory_space=pltpu.VMEM)
HELD = pl.BlockSpec(memory_space=pltpu.VMEM)
LIMIT = 30 * 2**20
UNROLL = (4, 8)
SMEM = pl.BlockSpec(memory_space=pltpu.SMEM)
ANY = pl.BlockSpec(memory_space=pl.ANY)
LEAVE = (9, 6, 7, 4, 5, 2, 3, 1)
STAY = (8, 14, 15, 12, 13, 10, 11, 0)
STEPS = (1, 2, 2, 2, 1)
FAR_STEPS = (1, 2, 2, 3)


def sibling(value):
    return lax.ppermute(value, "fsdp", CORES)


def around(value):
    return lax.ppermute(value, "fsdp", AROUND)


def across(value):
    return lax.ppermute(value, "tp", ((0, 1), (1, 0)))


def arrival_order(rows):
    index = lax.axis_index("fsdp")
    chip, core = index // 2, lax.rem(index, 2)
    place = jnp.where(lax.rem(chip, 2) == 0, chip // 2, 7 - chip // 2)
    sign = 1 - 2 * core

    def shard(step, which):
        at = lax.rem(place + step + 16, 8)
        return 2 * jnp.where(at < 4, 2 * at, 15 - 2 * at) + which

    order = [shard(0, core), shard(0, 1 - core)]
    for step in (1, 2, 3):
        order += [shard(-step * sign, core), shard(-step * sign, 1 - core)]
    order += [shard(4, core), shard(4, 1 - core)]
    for step in (1, 2, 3):
        order += [shard(step * sign, 1 - core), shard(step * sign, core)]
    return jnp.stack([rows * o for o in order] + [lax.axis_index("tp")]).astype(jnp.int32)


def after(value, *others):
    return lax.optimization_barrier((value, *others))[0]


def pack_kernel(query, key, value, out, up, down, early, late):
    cols = query.shape[1]
    for n, ref in enumerate((query, key, value)):
        early[:, n * cols : (n + 1) * cols] = ref[...]
    late[:, :cols] = out[...]
    late[:, cols : 2 * cols] = up[...]
    late[:, 2 * cols :] = down[...]


def all_after(values, *others):
    return lax.optimization_barrier((*values, *others))[: len(values)]


def ring_gather(early, late, tokens, prepare):
    rows = early.shape[0]
    first = [early, sibling(early)]
    here = [late, sibling(after(late, first[1]))]
    other_tokens = across(tokens)
    there = [across(after(late, other_tokens))]
    first.append(around(jnp.concatenate(first)))
    here.append(around(jnp.concatenate(here)))
    first.append(around(after(first[2], other_tokens)))
    here.append(around(here[2]))
    there.append(across(here[2]))
    first.append(around(after(first[3], there[0])))
    here.append(around(here[3]))
    there.append(across(here[3]))
    prepared = prepare(other_tokens)
    first.append(around(after(first[4][:rows], prepared, there[1])))
    here.append(around(here[4][:rows]))
    there.append(across(here[4]))
    there.append(across(here[5]))
    first += [sibling(after(first[5], here[5]))] + [sibling(first[n]) for n in (2, 3, 4)]
    return (first, here, there, prepared, other_tokens)


def swap_late(here, there, *wait):
    there = [there[0], sibling(there[0])] + there[1:]
    return [
        got + [sibling(after(got[n], *wait)) for n in (5, 2, 3, 4)] for got in (here, there)
    ]


def total(*terms):
    out = terms[0].astype(F32)
    for term in terms[1:]:
        out = out + term.astype(F32)
    return out


class Scatter:
    def __init__(self, parts, far=None, note=None):
        self.came_from = [sibling(part) for part in parts[:5]]
        self.stay = parts[5:]
        self.far = far
        self.rows, self.cols = self.stay[0].shape
        self.came = None
        self.note = note
        self.notes = []

    def step(self, number, *wait):
        terms = [self.stay[number], self.came_from[number]]
        rows = STEPS[number] * self.rows
        note = self.note is not None
        if self.far is not None:
            terms.append(self.far[number])
        if self.came is not None:
            terms.append(self.came)
        elif note:
            terms.append(self.note)
        if number == 0 and note:
            body = first_kernel
        else:
            body = functools.partial(add_kernel, number, note)
        out = struct(rows + (16 if note else 0), self.cols)
        sent = call(body, terms, [HELD] * len(terms), [(out, HELD)], [], 10**6)[0]
        self.sent = sent
        came = around(after(sent, *wait) if wait else sent)
        if note:
            self.notes.append(came[rows:])
        self.came = came
        return came

    def finish(self):
        rows = self.rows
        came = self.came
        terms = [self.stay[4], self.came_from[4], came[rows : 2 * rows], sibling(came[:rows])]
        if self.far is not None:
            terms.append(self.far[4])
        return total(*terms)


def dot(a, b, dims):
    return lax.dot_general(a, b, (dims, ((), ())), preferred_element_type=F32)


NN, NT = ((1,), (0,)), ((1,), (1,))


def put_shards(order, pieces, target, sems):
    rows = pieces[0].shape[0]
    copies = []
    for n, piece in enumerate(pieces[:2]):
        to = pl.ds(pl.multiple_of(order[n], 16), rows)
        copies.append(load(piece, target.at[to, :], sems.at[n]))
    n = 2
    for piece in pieces[2:]:
        for part in range(piece.shape[0] // rows):
            to = pl.ds(pl.multiple_of(order[n], 16), rows)
            target[to, :] = piece[part * rows : (part + 1) * rows, :]
            n += 1
    wait_all(copies)


def load(source, target, sem):
    copy = pltpu.make_async_copy(source, target, sem)
    copy.start()
    return copy


def wait_all(copies):
    for copy in copies:
        copy.wait()


def allowed_bias(starts, bias):
    length = bias.shape[0]
    key_pos = lax.broadcasted_iota(jnp.int32, (length, 1), 0)
    query_pos = lax.broadcasted_iota(jnp.int32, (1, length), 1)
    key_series = jnp.zeros((length, 1), jnp.int32)
    query_series = jnp.zeros((1, length), jnp.int32)
    for n in range(starts.shape[1]):
        key_series += (starts[0, n] <= key_pos).astype(jnp.int32)
        query_series += (starts[0, n] <= query_pos).astype(jnp.int32)
    allowed = (key_pos <= query_pos) & (key_series == query_series)
    bias[...] = jnp.where(allowed, 0.0, -1e30).astype(F32)


def attend_kernel(heads, order, starts, scaling, normed, *rest):
    pieces, rest = rest[:10], rest[10:]
    keep, send, logsum, proj_out, weights_out, proj_t, weights, bias, scores, mixed, sems = rest
    cols = heads * HD
    length = normed.shape[0]
    allowed_bias(starts, bias)
    put_shards(order, pieces, weights, sems)
    stores = [load(weights, weights_out, sems.at[2])]
    for n in range(3):
        part = dot(normed[...], weights[:, n * cols : (n + 1) * cols], NN)
        if n == 0:
            part = part * scaling[...]
        proj_t[n * cols : (n + 1) * cols, :] = part.astype(BF16).T
    stores.append(load(proj_t, proj_out, sems.at[3]))
    blocks = ((0, length // 2), (length // 2, length))

    def rows(n, h):
        return pl.ds(pl.multiple_of(n * cols + h * HD, 16), HD)

    def one_head(h, slot):
        query = proj_t[rows(0, h), :]
        key = proj_t[rows(1, h), :].T
        value = proj_t[rows(2, h), :]
        for start, stop in blocks:
            scores[slot, :stop, start:stop] = dot(key[:stop], query[:, start:stop], NN)
        for start, stop in blocks:
            part = scores[slot, :stop, start:stop] + bias[:stop, start:stop]
            row_max = jnp.max(part, axis=0, keepdims=True)
            exponent = jnp.exp(part - row_max)
            total = jnp.sum(exponent, axis=0, keepdims=True)
            soft_b = (exponent * (1.0 / total)).astype(BF16)
            mixed[rows(0, h), start:stop] = dot(value[:, :stop], soft_b, NN).astype(BF16)
            logsum[h, :, start:stop] = row_max + jnp.log(total)

    @pl.loop(0, heads // UNROLL[0])
    def _(block):
        for n in range(UNROLL[0]):
            one_head(block * UNROLL[0] + n, n)

    half = order[16]
    low, high = mixed[:, : length // 2], mixed[:, length // 2 :]
    keep[...] = jnp.where(half == 0, low, high)
    send[...] = jnp.where(half == 0, high, low)
    wait_all(stores)


def assemble_kernel(order, *rest):
    here, there, (weights, sems) = rest[:10], rest[10:20], rest[20:]
    put_shards(order, here, weights.at[0], sems)
    put_shards(order, there, weights.at[1], sems)


def middle_kernel(
    tokens, cot, gain, keep, came, weights,
    dkeep, dsend, hidden_o, dup_o, normed_o, dattn_o, mixed_o, middle_o, dgain_o, dmiddle_out,
    dhidden, dmiddle_o, sem,
):
    cols = keep.shape[0]
    out, up, down = (slice(n * cols, (n + 1) * cols) for n in range(3))

    def half(n):
        return pl.ds(pl.multiple_of(n * cols, 128), cols)

    mixed_o[:, :cols] = keep[...].T
    mixed_o[:, cols:] = came[...].T
    middle_o[...] = tokens[...].astype(F32)

    @pl.loop(0, 2)
    def _(n):
        middle_o[...] += dot(mixed_o[:, half(n)], weights[n, :, out], NT)
        dhidden[:, half(n)] = dot(cot[...], weights[n, :, down], NN)

    middle = middle_o[...]
    scale = lax.rsqrt(jnp.mean(middle * middle, axis=-1, keepdims=True) + epsilon)
    normed_o[...] = (middle * scale * gain[...]).astype(BF16)

    @pl.loop(0, 2)
    def _(n):
        u = dot(normed_o[...], weights[n, :, up], NN)
        root = math.sqrt(2.0 / math.pi)
        square = u * u
        tanh = jnp.tanh(root * u * (1.0 + 0.044715 * square))
        gate = 0.5 * (1.0 + tanh)
        hidden_o[:, half(n)] = (u * gate).astype(BF16)
        slope = gate + 0.5 * u * (1.0 - tanh * tanh) * (root * (1.0 + 3 * 0.044715 * square))
        dup_o[:, half(n)] = (dhidden[:, half(n)] * slope).astype(BF16)

    dmiddle_o[...] = jnp.zeros_like(dmiddle_o)

    @pl.loop(0, 2)
    def _(n):
        dmiddle_o[...] += dot(dup_o[:, half(n)], weights[n, :, up], NT)

    dnormed = dmiddle_o[...]
    middle = middle_o[...]
    dgain_o[...] = jnp.sum(dnormed * middle * scale, axis=0, keepdims=True)
    weighted = dnormed * gain[...]
    mean = jnp.mean(weighted * middle, axis=-1, keepdims=True)
    dmiddle = cot[...].astype(F32) + scale * weighted - middle * (scale * scale * scale * mean)
    dmiddle_o[...] = dmiddle
    store = load(dmiddle_o, dmiddle_out, sem)
    dattn_o[...] = dmiddle.astype(BF16)
    for n, ref in enumerate((dkeep, dsend)):
        ref[...] = dot(dattn_o[...], weights[n, :, out], NN).astype(BF16).T
    store.wait()


def by_arrival(order, source_t, target, rows):
    for n, which in enumerate(LEAVE + STAY):
        target[n * rows : (n + 1) * rows, :] = source_t[
            pl.ds(pl.multiple_of(order[which], 16), rows), :
        ]


def split_rows(steps, rows, at=0):
    out = []
    for count in steps:
        out.append(slice(at, at + count * rows))
        at += count * rows
    return out


def late_grads_kernel(order, hidden, dup, normed, dattn, mixed, middle, weights, cot, *rest):
    outs, (grads, result, left_t, left, sems) = rest[:19], rest[19:]
    cols = dup.shape[1] // 2
    rows = dup.shape[1] // 16
    pairs = ((dattn, mixed), (normed, dup), (cot, hidden))
    for n, (a, _) in enumerate(pairs):
        left_t[n, :, :] = a[...].T
        by_arrival(order, left_t.at[n], left.at[n], rows)
    stores = []
    for leaves in range(2):
        top = leaves * 8 * rows
        part = slice(top, top + 8 * rows)
        for side, steps, start in ((1, FAR_STEPS, 10), (0, STEPS, 0)):
            for n, (_, b) in enumerate(pairs):
                grads[side, part, n * cols : (n + 1) * cols] = dot(
                    left[n, part, :], b[:, side * cols : (side + 1) * cols], NN
                ).astype(BF16)
            start += leaves * len(steps)
            for k, at in enumerate(split_rows(steps, rows, top)):
                stores.append(load(grads.at[side, at, :], outs[start + k], sems.at[start + k]))
    total = middle[...]
    for side in range(2):
        at = slice(side * cols, (side + 1) * cols)
        total = total + dot(hidden[:, at], weights[side, :, 2 * cols :], NT)
    result[...] = total.astype(BF16)
    stores.append(load(result, outs[18], sems.at[18]))
    wait_all(stores)


def attend_back_kernel(
    heads, order, starts, scaling_col, keep, came, logsum, proj_in, weights_in, tokens_in, other_in,
    dscaling, dgain, dproj_out, keep_out, send_out,
    weights, proj_t, bias, dmixed, dproj_t, scores, dsofts, dproj, kept, sent, tokens, sems,
):
    fetch = load(proj_in, proj_t, sems.at[0])
    fetch_late = [
        load(weights_in, weights, sems.at[1]),
        load(tokens_in, tokens.at[0], sems.at[2]),
        load(other_in, tokens.at[1], sems.at[3]),
    ]
    cols = heads * HD
    length = proj_t.shape[1]
    rows = length // 2
    allowed_bias(starts, bias)
    half = order[16]
    dmixed[:, :rows] = jnp.where(half == 0, keep[...], came[...])
    dmixed[:, rows:] = jnp.where(half == 0, came[...], keep[...])
    fetch.wait()
    dscaling[...] = jnp.zeros_like(dscaling)

    def place(n, h):
        return pl.ds(pl.multiple_of(n * cols + h * HD, 16), HD)

    def one_head(h, slot):
        query = proj_t[place(0, h), :]
        key_t = proj_t[place(1, h), :]
        key = key_t.T
        value = proj_t[place(2, h), :].T
        grad = dmixed[place(0, h), :]
        for start, stop in ((0, rows), (rows, length)):
            scores[slot, :stop, start:stop] = dot(key[:stop], query[:, start:stop], NN)
            dsofts[slot, :stop, start:stop] = dot(value[:stop], grad[:, start:stop], NN)
        parts = []
        for start, stop in ((rows, length), (0, rows)):
            soft = scores[slot, :stop, start:stop] + bias[:stop, start:stop]
            soft = jnp.exp(soft - logsum[h, :, start:stop])
            dsoft = dsofts[slot, :stop, start:stop]
            inner = jnp.sum(soft * dsoft, axis=0, keepdims=True)
            dscores = (soft * (dsoft - inner)).astype(BF16)
            dquery = dot(key_t[:, :stop], dscores, NN)
            dscaling[...] += jnp.sum(
                dquery * query[:, start:stop].astype(F32), axis=1, keepdims=True
            )
            dproj_t[place(0, h), start:stop] = (dquery * scaling_col[...]).astype(BF16)
            parts.append(
                (dot(dscores, query[:, start:stop], NT), dot(soft.astype(BF16), grad[:, start:stop], NT))
            )
        for n in range(2):
            both = jnp.concatenate([parts[0][n][:rows] + parts[1][n], parts[0][n][rows:]], axis=0)
            dproj_t[place(n + 1, h), :] = both.astype(BF16).T

    @pl.loop(0, heads // UNROLL[1])
    def _(block):
        for n in range(UNROLL[1]):
            one_head(block * UNROLL[1] + n, n % 2)

    dproj[...] = dproj_t[...].T
    stores = [load(dproj, dproj_out, sems.at[4])]
    wait_all(fetch_late)
    parts = []
    total = jnp.zeros(dgain.shape, F32)
    for n in range(2):
        part = dot(dproj[n * rows : (n + 1) * rows, :], weights[...], NT)
        resid = jnp.where(half == n, tokens[0], tokens[1]).astype(F32)
        scale = lax.rsqrt(jnp.mean(resid * resid, axis=-1, keepdims=True) + epsilon)
        total = total + jnp.sum(part * resid * scale, axis=0, keepdims=True)
        parts.append(part)
    dgain[...] = total
    sent[...] = jnp.where(half == 0, parts[1], parts[0]).astype(BF16)
    stores.append(load(sent, send_out, sems.at[5]))
    kept[...] = jnp.where(half == 0, parts[0], parts[1])
    stores.append(load(kept, keep_out, sems.at[6]))
    wait_all(stores)


def early_grads_kernel(order, normed, dproj_in, *rest):
    outs, (dproj, grads, left_t, left, sems) = rest[:10], rest[10:]
    fetch = load(dproj_in, dproj, sems.at[10])
    rows = normed.shape[1] // 16
    left_t[...] = normed[...].T
    by_arrival(order, left_t, left, rows)
    fetch.wait()
    stores = []
    for leaves in range(2):
        top = leaves * 8 * rows
        part = slice(top, top + 8 * rows)
        grads[part, :] = dot(left[part, :], dproj[...], NN).astype(BF16)
        for k, at in enumerate(split_rows(STEPS, rows, top)):
            n = 5 * leaves + k
            stores.append(load(grads.at[at, :], outs[n], sems.at[n]))
    wait_all(stores)


def first_kernel(stay, came, note, out):
    rows = stay.shape[0]
    out[:rows, :] = (stay[...].astype(F32) + came[...].astype(F32)).astype(BF16)
    out[rows:, :] = note[...]


def add_kernel(number, note, *rest):
    *terms, out = rest
    rows = terms[0].shape[0]
    late = terms.pop() if number > 0 else None
    part = terms[0][...].astype(F32)
    for term in terms[1:]:
        part = part + term[...].astype(F32)
    if number == 1:
        half = rows // 2
        out[:half, :] = part[:half].astype(BF16)
        out[half:rows, :] = (part[half:] + late[:half, :].astype(F32)).astype(BF16)
    else:
        if late is not None:
            part = part + late[:rows, :].astype(F32)
        out[:rows, :] = part.astype(BF16)
    if note:
        out[rows:, :] = late[late.shape[0] - 16 :, :]


def pair_kernel(one, other, out):
    out[...] = (one[...].astype(F32) + other[...].astype(F32)).astype(BF16)


def struct(*shape, kind=BF16):
    return jax.ShapeDtypeStruct(shape, kind)


def call(body, inputs, spaces, outputs, scratch, flops):
    place = {id(HELD): pltpu.VMEM, id(ANY): pltpu.HBM, id(VMEM): pltpu.HBM}
    inputs = [
        pltpu.with_memory_space_constraint(value, place[id(space)]) if id(space) in place else value
        for value, space in zip(inputs, spaces)
    ]
    return pl.pallas_call(
        body,
        out_shape=[place[id(space)](out.shape, out.dtype) for out, space in outputs],
        in_specs=[VMEM if space is HELD else space for space in spaces],
        out_specs=[VMEM if space is HELD else space for _, space in outputs],
        scratch_shapes=scratch,
        compiler_params=pltpu.CompilerParams(vmem_limit_bytes=LIMIT),
        cost_estimate=pl.CostEstimate(flops=flops * 4, bytes_accessed=2**22, transcendentals=0),
    )(*inputs)


def in_order(half, own, other, axis=0):
    return jnp.where(
        half == 0,
        jnp.concatenate([own, other], axis=axis),
        jnp.concatenate([other, own], axis=axis),
    )


def on_slice(
    tokens,
    seg_starts,
    gain_attn,
    gain_mlp,
    query_scale,
    w_query,
    w_key,
    w_value,
    w_out,
    w_up,
    w_down,
    cotangent,
):
    half = lax.axis_index("tp")
    rows, width = tokens.shape
    shard, cols = w_query.shape
    length = 2 * rows
    heads = cols // HD
    dma = pltpu.SemaphoreType.DMA
    order = arrival_order(shard)
    early, late = call(
        pack_kernel,
        [w_query, w_key, w_value, w_out.T, w_up, w_down.T],
        [VMEM] * 6,
        [(struct(shard, 3 * cols), VMEM)] * 2,
        [],
        10**6,
    )

    def prepare(other_tokens):
        row_tokens = in_order(half, tokens, other_tokens).astype(F32)
        return (row_tokens * inverse_rms(row_tokens) * gain_attn).astype(BF16)

    first, here, there, normed, other_tokens = ring_gather(early, late, tokens, prepare)
    scaling = softplus_unit / math.sqrt(HD) * jax.nn.softplus(query_scale)
    keep, send, logsum, proj_t, w_in = call(
        functools.partial(attend_kernel, heads),
        [after(order, there[2]), seg_starts, jnp.tile(scaling, heads)[None, :], normed]
        + first,
        [SMEM] * 2 + [HELD] * 2 + [ANY] * 2 + [HELD] * 8,
        [
            (struct(cols, rows), HELD),
            (struct(cols, rows), HELD),
            (struct(heads, 1, length, kind=F32), HELD),
            (struct(3 * cols, length), ANY),
            (struct(width, 3 * cols), ANY),
        ],
        [
            pltpu.VMEM((3 * cols, length), BF16),
            pltpu.VMEM((width, 3 * cols), BF16),
            pltpu.VMEM((length, length), F32),
            pltpu.VMEM((UNROLL[0], length, length), F32),
            pltpu.VMEM((cols, length), BF16),
            dma((4,)),
        ],
        8 * 10**9,
    )
    came = across(send)
    here, there = swap_late(here, there, logsum)
    w_late = call(
        assemble_kernel,
        [order, *here, *there],
        [SMEM] + ([ANY] * 2 + [HELD] * 8) * 2,
        [(struct(2, width, 3 * cols), HELD)],
        [dma((2,))],
        10**6,
    )[0]
    act = struct(rows, width)
    dkeep, dsend, *saved, dgain_two, dmiddle = call(
        middle_kernel,
        [tokens, cotangent, gain_mlp[None, :], keep, came, w_late],
        [HELD] * 6,
        [(struct(cols, rows), HELD)] * 2
        + [(act, HELD)] * 5
        + [
            (struct(rows, width, kind=F32), HELD),
            (struct(1, width, kind=F32), HELD),
            (struct(rows, width, kind=F32), ANY),
        ],
        [pltpu.VMEM((rows, width), F32), pltpu.VMEM((rows, width), F32), dma],
        8 * 10**9,
    )
    dcame = across(dsend)
    *parts, result = call(
        late_grads_kernel,
        [order, *saved, w_late, cotangent],
        [SMEM] + [HELD] * 8,
        [(struct(n * shard, 3 * cols), ANY) for n in STEPS * 2 + FAR_STEPS * 2] + [(act, ANY)],
        [
            pltpu.VMEM((2, width, 3 * cols), BF16),
            pltpu.VMEM((rows, width), BF16),
            pltpu.VMEM((3, width, rows), BF16),
            pltpu.VMEM((3, width, rows), BF16),
            dma((19,)),
        ],
        6 * 10**9,
    )
    *parts, result = all_after((*parts, result), dcame)
    far, far_sent = [], []
    for n, steps in enumerate(FAR_STEPS):
        pair = [parts[14 + n], sibling(parts[10 + n])]
        sent = call(pair_kernel, pair, [HELD] * 2, [(struct(steps * shard, 3 * cols), HELD)], [], 10**6)
        far_sent += sent
        far.append(across(sent[0]))
    far_last = far.pop()
    far += [far_last[: 2 * shard], far_last[2 * shard :]]
    late_sum = Scatter(parts[:10], far)
    late_one = late_sum.step(0)
    dscaling, dgain_one, dproj, dnormed, dnormed_send = call(
        functools.partial(attend_back_kernel, heads),
        [
            after(order, late_sum.came_from[0]),
            seg_starts,
            scaling[:, None],
            dkeep,
            dcame,
            logsum,
            proj_t,
            w_in,
            tokens,
            other_tokens,
        ],
        [SMEM] * 2 + [HELD] * 4 + [ANY] * 4,
        [
            (struct(HD, 1, kind=F32), HELD),
            (struct(1, width, kind=F32), HELD),
            (struct(length, 3 * cols), ANY),
            (struct(rows, width, kind=F32), ANY),
            (act, ANY),
        ],
        [
            pltpu.VMEM((width, 3 * cols), BF16),
            pltpu.VMEM((3 * cols, length), BF16),
            pltpu.VMEM((length, length), F32),
            pltpu.VMEM((cols, length), BF16),
            pltpu.VMEM((3 * cols, length), BF16),
            pltpu.VMEM((2, length, length), F32),
            pltpu.VMEM((2, length, length), F32),
            pltpu.VMEM((length, 3 * cols), BF16),
            pltpu.VMEM((rows, width), F32),
            pltpu.VMEM((rows, width), BF16),
            pltpu.VMEM((2, rows, width), BF16),
            dma((7,)),
        ],
        12 * 10**9,
    )
    dscaling, dgain_one, dproj, dnormed, dnormed_send = all_after(
        (dscaling, dgain_one, dproj, dnormed, dnormed_send), *far[:2]
    )
    dscale_param = (
        dscaling[:, 0] / scaling * (softplus_unit / math.sqrt(HD)) * jax.nn.sigmoid(query_scale)
    )
    note = jnp.concatenate(
        [
            jnp.concatenate([dgain_one, jnp.pad(dscale_param[None, :], ((0, 0), (0, cols - HD)))], axis=1),
            jnp.pad(dgain_two, ((0, 0), (0, cols))),
        ]
    )
    parts = call(
        early_grads_kernel,
        [after(order, far_sent[2]), normed, dproj],
        [SMEM, HELD, ANY],
        [(struct(n * shard, 3 * cols), ANY) for n in STEPS + STEPS],
        [
            pltpu.VMEM((length, 3 * cols), BF16),
            pltpu.VMEM((width, 3 * cols), BF16),
            pltpu.VMEM((width, length), BF16),
            pltpu.VMEM((width, length), BF16),
            dma((11,)),
        ],
        5 * 10**9,
    )
    note = note + sibling(after(note, parts[1]))
    high = lax.reduce_precision(note, 8, 7)
    coded = jnp.concatenate([high, note - high, jnp.zeros((12, 3 * cols), F32)]).astype(BF16)
    parts = all_after(parts, late_one)
    late_two = late_sum.step(1)
    early_sum = Scatter(parts, note=coded)
    early_sum.step(0)
    late_three = late_sum.step(2)
    early_sum.came = after(early_sum.came, late_two)
    early_sum.step(1)
    late_four = late_sum.step(3)
    early_three = early_sum.step(2)
    dnormed = dnormed + after(across(dnormed_send), early_three).astype(F32)
    resid = tokens.astype(F32)
    dresid_one, _ = norm_backward(resid, inverse_rms(resid), gain_attn, dnormed)
    early_sum.came = after(early_sum.came, late_three, far[3])
    early_sum.step(3)
    late_sum.came = after(late_sum.came, early_sum.sent)
    dlate = late_sum.finish()
    din = early_sum.finish()
    mine = early_sum.notes
    core = lax.rem(lax.axis_index("fsdp"), 2)
    heard = total(*mine[:3]) + jnp.where(core == 0, 1.0, 0.0) * mine[3].astype(F32)
    heard = heard[:2] + heard[2:4]
    heard = heard + sibling(heard)
    small = note + heard
    small = small + across(small)
    return (
        result,
        dmiddle + dresid_one,
        small[0, :width],
        small[1, :width],
        small[0, width : width + HD],
        din[:, :cols],
        din[:, cols : 2 * cols],
        din[:, 2 * cols :],
        dlate[:, :cols].T,
        dlate[:, cols : 2 * cols],
        dlate[:, 2 * cols :].T,
    )


def solution(mesh):
    body = on_slice if dict(mesh.shape) == {"fsdp": 16, "tp": 2} else on_device
    placed = (
        P(("fsdp", "tp"), None),
        P("fsdp", None),
        P(),
        P(),
        P(),
        P("fsdp", "tp"),
        P("fsdp", "tp"),
        P("fsdp", "tp"),
        P("tp", "fsdp"),
        P("fsdp", "tp"),
        P("tp", "fsdp"),
        P(("fsdp", "tp"), None),
    )
    return jax.shard_map(
        body,
        mesh=mesh,
        in_specs=placed,
        out_specs=(
            P(("fsdp", "tp"), None),
            P(("fsdp", "tp"), None),
            P(),
            P(),
            P(),
            P("fsdp", "tp"),
            P("fsdp", "tp"),
            P("fsdp", "tp"),
            P("tp", "fsdp"),
            P("fsdp", "tp"),
            P("tp", "fsdp"),
        ),
        check_vma=False,
    )
```

```python
import functools
import math

import jax
import jax.numpy as jnp
from jax import lax
from jax.experimental import pallas as pl
from jax.experimental.pallas import tpu as pltpu
from jax.sharding import PartitionSpec as P

HD = 80


epsilon = 1e-06
softplus_unit = 1.442695041


def inverse_rms(values):
    return lax.rsqrt(jnp.mean(values * values, axis=-1, keepdims=True) + epsilon)


def norm_backward(resid, inv_scale, gain, dnormed):
    weighted = dnormed * gain
    cubed = inv_scale * inv_scale * inv_scale
    dresid = inv_scale * weighted - resid * cubed * jnp.mean(
        weighted * resid, axis=-1, keepdims=True
    )
    dgain = jnp.sum(dnormed * resid * inv_scale, axis=0)
    return (dresid, dgain)


def segment_ids(starts, length):
    positions = jnp.arange(length, dtype=jnp.int32)
    inside = (starts[None, :] <= positions[:, None]).astype(jnp.int32)
    return (positions, jnp.sum(inside, axis=1) - 1)


def block_scores(query_blk, block_pos, block_series, key_b, positions, series):
    scores = jnp.einsum("qhd,khd->hqk", query_blk, key_b, preferred_element_type=jnp.float32)
    allowed = (positions[None, :] <= block_pos[:, None]) & (
        series[None, :] == block_series[:, None]
    )
    return jnp.where(allowed[None], scores, -1e30)


def attend_forward(query_b, key_b, value_b, positions, series, block_rows):
    num_blocks = query_b.shape[0] // block_rows
    local_heads = query_b.shape[1]

    def one_block(inputs):
        query_blk, block_pos, block_series = inputs
        scores = block_scores(query_blk, block_pos, block_series, key_b, positions, series)
        row_max = jnp.max(scores, axis=-1, keepdims=True)
        exponent = jnp.exp(scores - row_max)
        total = jnp.sum(exponent, axis=-1, keepdims=True)
        soft_b = (exponent / total).astype(jnp.bfloat16)
        mixed = jnp.einsum("hqk,khd->qhd", soft_b, value_b, preferred_element_type=jnp.float32)
        return (mixed, row_max + jnp.log(total))

    mixed, logsum = lax.map(
        one_block,
        (
            query_b.reshape(num_blocks, block_rows, local_heads, HD),
            positions.reshape(num_blocks, block_rows),
            series.reshape(num_blocks, block_rows),
        ),
    )
    return (mixed.reshape(query_b.shape[0], local_heads * HD), logsum)


def attend_backward(query_b, key_b, value_b, dmixed, logsum, positions, series, block_rows):
    num_blocks = query_b.shape[0] // block_rows
    local_heads = query_b.shape[1]

    def one_block(carry, inputs):
        dkey, dvalue = carry
        query_blk, dmixed_blk, block_pos, block_series, logsum_blk = inputs
        scores = block_scores(query_blk, block_pos, block_series, key_b, positions, series)
        soft = jnp.exp(scores - logsum_blk)
        dsoft = jnp.einsum("qhd,khd->hqk", dmixed_blk, value_b, preferred_element_type=jnp.float32)
        inner = jnp.sum(soft * dsoft, axis=-1, keepdims=True)
        dscores = (soft * (dsoft - inner)).astype(jnp.bfloat16)
        dquery_blk = jnp.einsum("hqk,khd->qhd", dscores, key_b, preferred_element_type=jnp.float32)
        dkey = dkey + jnp.einsum(
            "hqk,qhd->khd", dscores, query_blk, preferred_element_type=jnp.float32
        )
        dvalue = dvalue + jnp.einsum(
            "hqk,qhd->khd",
            soft.astype(jnp.bfloat16),
            dmixed_blk,
            preferred_element_type=jnp.float32,
        )
        return ((dkey, dvalue), dquery_blk)

    zeros = jnp.zeros(key_b.shape, jnp.float32)
    inputs = (
        query_b.reshape(num_blocks, block_rows, local_heads, HD),
        dmixed.reshape(num_blocks, block_rows, local_heads, HD),
        positions.reshape(num_blocks, block_rows),
        series.reshape(num_blocks, block_rows),
        logsum,
    )
    (dkey, dvalue), dquery = lax.scan(one_block, (zeros, zeros), inputs)
    return (dquery.reshape(query_b.shape), dkey, dvalue)


def on_device(
    tokens,
    seg_starts,
    gain_attn,
    gain_mlp,
    query_scale,
    w_query,
    w_key,
    w_value,
    w_out,
    w_up,
    w_down,
    cotangent,
):
    gathered = (
        lax.all_gather(w_query, "fsdp", axis=0, tiled=True),
        lax.all_gather(w_key, "fsdp", axis=0, tiled=True),
        lax.all_gather(w_value, "fsdp", axis=0, tiled=True),
        lax.all_gather(w_out, "fsdp", axis=1, tiled=True),
        lax.all_gather(w_up, "fsdp", axis=0, tiled=True),
        lax.all_gather(w_down, "fsdp", axis=1, tiled=True),
    )
    full_query, full_key, full_value, full_out, full_up, full_down = gathered
    local_rows = tokens.shape[0]
    row_length = local_rows * lax.axis_size("tp")
    block_rows = min(512, row_length)
    local_heads = full_query.shape[1] // HD
    positions, series = segment_ids(seg_starts[0], row_length)
    resid = tokens.astype(jnp.float32)
    scale_one = inverse_rms(resid)
    normed_one = (resid * scale_one * gain_attn).astype(jnp.bfloat16)
    gathered_one = lax.all_gather(normed_one, "tp", axis=0, tiled=True)
    query = jnp.dot(gathered_one, full_query, preferred_element_type=jnp.float32).reshape(
        row_length, local_heads, HD
    )
    scaling = softplus_unit / math.sqrt(HD) * jax.nn.softplus(query_scale)
    query_b = (query * scaling).astype(jnp.bfloat16)
    key_b = (
        jnp.dot(gathered_one, full_key, preferred_element_type=jnp.float32)
        .astype(jnp.bfloat16)
        .reshape(row_length, local_heads, HD)
    )
    value_b = (
        jnp.dot(gathered_one, full_value, preferred_element_type=jnp.float32)
        .astype(jnp.bfloat16)
        .reshape(row_length, local_heads, HD)
    )
    mixed, logsum = attend_forward(query_b, key_b, value_b, positions, series, block_rows)
    mixed_b = mixed.astype(jnp.bfloat16)
    attn_part = jnp.dot(mixed_b, full_out, preferred_element_type=jnp.float32)
    middle = resid + lax.psum_scatter(attn_part, "tp", scatter_dimension=0, tiled=True)
    scale_two = inverse_rms(middle)
    normed_two = (middle * scale_two * gain_mlp).astype(jnp.bfloat16)
    wide_up, wide_down = (full_up, full_down)
    mlp_input = lax.all_gather(normed_two, "tp", axis=0, tiled=True)
    upward = jnp.dot(mlp_input, wide_up, preferred_element_type=jnp.float32)
    activated, gelu_back = jax.vjp(jax.nn.gelu, upward)
    hidden_b = activated.astype(jnp.bfloat16)
    mlp_part = jnp.dot(hidden_b, wide_down, preferred_element_type=jnp.float32)
    mlp_sum = lax.psum_scatter(
        mlp_part.astype(jnp.bfloat16), "tp", scatter_dimension=0, tiled=True
    ).astype(jnp.float32)
    result = (middle + mlp_sum).astype(jnp.bfloat16)
    dlower = lax.all_gather(cotangent, "tp", axis=0, tiled=True)
    grad_down_here = jnp.einsum("rf,rd->fd", hidden_b, dlower, preferred_element_type=jnp.float32)
    dhidden = jnp.einsum("rd,fd->rf", dlower, wide_down, preferred_element_type=jnp.float32)
    dupward = gelu_back(dhidden)[0].astype(jnp.bfloat16)
    grad_up_here = jnp.einsum("rd,rf->df", mlp_input, dupward, preferred_element_type=jnp.float32)
    dnorm_part = jnp.einsum("rf,df->rd", dupward, wide_up, preferred_element_type=jnp.float32)
    dnormed_two = lax.psum_scatter(dnorm_part, "tp", scatter_dimension=0, tiled=True)
    grad_up_part, grad_down_part = (grad_up_here, grad_down_here)
    dresid_two, dgain_two = norm_backward(middle, scale_two, gain_mlp, dnormed_two)
    dmiddle = cotangent.astype(jnp.float32) + dresid_two
    dattn = lax.all_gather(dmiddle.astype(jnp.bfloat16), "tp", axis=0, tiled=True)
    grad_out_part = jnp.einsum("rh,rd->hd", mixed_b, dattn, preferred_element_type=jnp.float32)
    dmixed = jnp.einsum("rd,hd->rh", dattn, full_out, preferred_element_type=jnp.float32).astype(
        jnp.bfloat16
    )
    dquery_scaled, dkey, dvalue = attend_backward(
        query_b, key_b, value_b, dmixed, logsum, positions, series, block_rows
    )
    dscaling = jnp.sum(dquery_scaled * query, axis=(0, 1))
    dquery = (dquery_scaled * scaling).astype(jnp.bfloat16).reshape(row_length, local_heads * HD)
    dkey_b = dkey.astype(jnp.bfloat16).reshape(row_length, local_heads * HD)
    dvalue_b = dvalue.astype(jnp.bfloat16).reshape(row_length, local_heads * HD)
    grad_query_part = jnp.einsum(
        "rd,rh->dh", gathered_one, dquery, preferred_element_type=jnp.float32
    )
    grad_key_part = jnp.einsum(
        "rd,rh->dh", gathered_one, dkey_b, preferred_element_type=jnp.float32
    )
    grad_value_part = jnp.einsum(
        "rd,rh->dh", gathered_one, dvalue_b, preferred_element_type=jnp.float32
    )
    dnorm_one_part = jnp.einsum("rh,dh->rd", dquery, full_query, preferred_element_type=jnp.float32)
    dnorm_one_part = dnorm_one_part + jnp.einsum(
        "rh,dh->rd", dkey_b, full_key, preferred_element_type=jnp.float32
    )
    dnorm_one_part = dnorm_one_part + jnp.einsum(
        "rh,dh->rd", dvalue_b, full_value, preferred_element_type=jnp.float32
    )
    dnormed_one = lax.psum_scatter(dnorm_one_part, "tp", scatter_dimension=0, tiled=True)
    dresid_one, dgain_one = norm_backward(resid, scale_one, gain_attn, dnormed_one)
    grad_tokens = dmiddle + dresid_one
    summed = (
        lax.psum_scatter(grad_query_part, "fsdp", scatter_dimension=0, tiled=True),
        lax.psum_scatter(grad_key_part, "fsdp", scatter_dimension=0, tiled=True),
        lax.psum_scatter(grad_value_part, "fsdp", scatter_dimension=0, tiled=True),
        lax.psum_scatter(grad_out_part, "fsdp", scatter_dimension=1, tiled=True),
        lax.psum_scatter(grad_up_part, "fsdp", scatter_dimension=0, tiled=True),
        lax.psum_scatter(grad_down_part, "fsdp", scatter_dimension=1, tiled=True),
    )
    dscale_param = dscaling * (softplus_unit / math.sqrt(HD)) * jax.nn.sigmoid(query_scale)
    grad_gain_attn, grad_gain_mlp, grad_query_scale = lax.psum(
        (dgain_one, dgain_two, dscale_param), ("fsdp", "tp")
    )
    return (
        result,
        grad_tokens,
        grad_gain_attn,
        grad_gain_mlp,
        grad_query_scale,
        summed[0],
        summed[1],
        summed[2],
        summed[3],
        summed[4],
        summed[5],
    )


BF16, F32 = jnp.bfloat16, jnp.float32
RING = (0, 2, 4, 6, 7, 5, 3, 1)
CORES = tuple((i, i ^ 1) for i in range(16))
AROUND = tuple((2 * RING[i], 2 * RING[(i + 1) % 8]) for i in range(8)) + tuple(
    (2 * RING[i] + 1, 2 * RING[(i + 7) % 8] + 1) for i in range(8)
)
VMEM = pl.BlockSpec(memory_space=pltpu.VMEM)
HELD = pl.BlockSpec(memory_space=pltpu.VMEM)
LIMIT = 24 * 2**20
UNROLL = (4, 8)
SMEM = pl.BlockSpec(memory_space=pltpu.SMEM)
ANY = pl.BlockSpec(memory_space=pl.ANY)
LEAVE = (9, 6, 7, 4, 5, 2, 3, 1)
STAY = (8, 14, 15, 12, 13, 10, 11, 0)
STEPS = (1, 2, 2, 2, 1)
FAR_STEPS = (1, 2, 2, 3)


def sibling(value):
    return lax.ppermute(value, "fsdp", CORES)


def around(value):
    return lax.ppermute(value, "fsdp", AROUND)


def across(value):
    return lax.ppermute(value, "tp", ((0, 1), (1, 0)))


def arrival_order(rows):
    index = lax.axis_index("fsdp")
    chip, core = index // 2, lax.rem(index, 2)
    place = jnp.where(lax.rem(chip, 2) == 0, chip // 2, 7 - chip // 2)
    sign = 1 - 2 * core

    def shard(step, which):
        at = lax.rem(place + step + 16, 8)
        return 2 * jnp.where(at < 4, 2 * at, 15 - 2 * at) + which

    order = [shard(0, core), shard(0, 1 - core)]
    for step in (1, 2, 3):
        order += [shard(-step * sign, core), shard(-step * sign, 1 - core)]
    order += [shard(4, core), shard(4, 1 - core)]
    for step in (1, 2, 3):
        order += [shard(step * sign, 1 - core), shard(step * sign, core)]
    return jnp.stack([rows * o for o in order] + [lax.axis_index("tp")]).astype(jnp.int32)


def after(value, *others):
    return lax.optimization_barrier((value, *others))[0]


def pack_kernel(query, key, value, out, up, down, early, late):
    cols = query.shape[1]
    for n, ref in enumerate((query, key, value)):
        early[:, n * cols : (n + 1) * cols] = ref[...]
    late[:, :cols] = out[...]
    late[:, cols : 2 * cols] = up[...]
    late[:, 2 * cols :] = down[...]


def all_after(values, *others):
    return lax.optimization_barrier((*values, *others))[: len(values)]


def ring_gather(early, late, tokens, prepare):
    rows = early.shape[0]
    first = [early, sibling(early)]
    here = [late, sibling(after(late, first[1]))]
    other_tokens = across(tokens)
    there = [across(after(late, other_tokens))]
    first.append(around(jnp.concatenate(first)))
    here.append(around(jnp.concatenate(here)))
    first.append(around(after(first[2], other_tokens)))
    here.append(around(here[2]))
    there.append(across(here[2]))
    first.append(around(after(first[3], there[0])))
    here.append(around(here[3]))
    there.append(across(here[3]))
    prepared = prepare(other_tokens)
    first.append(around(after(first[4][:rows], prepared, there[1])))
    here.append(around(here[4][:rows]))
    there.append(across(here[4]))
    there.append(across(here[5]))
    first += [sibling(after(first[5], here[5]))] + [sibling(first[n]) for n in (2, 3, 4)]
    return (first, here, there, prepared, other_tokens)


def swap_late(here, there, *wait):
    there = [there[0], sibling(there[0])] + there[1:]
    return [
        got + [sibling(after(got[n], *wait)) for n in (5, 2, 3, 4)] for got in (here, there)
    ]


def total(*terms):
    out = terms[0].astype(F32)
    for term in terms[1:]:
        out = out + term.astype(F32)
    return out


class Scatter:
    def __init__(self, parts, far=None, note=None):
        self.came_from = [sibling(part) for part in parts[:5]]
        self.stay = parts[5:]
        self.far = far
        self.rows, self.cols = self.stay[0].shape
        self.came = None
        self.note = note
        self.notes = []

    def step(self, number, *wait):
        terms = [self.stay[number], self.came_from[number]]
        rows = STEPS[number] * self.rows
        note = self.note is not None
        if self.far is not None:
            terms.append(self.far[number])
        if self.came is not None:
            terms.append(self.came)
        elif note:
            terms.append(self.note)
        if number == 0 and note:
            body = first_kernel
        else:
            body = functools.partial(add_kernel, number, note)
        out = struct(rows + (16 if note else 0), self.cols)
        sent = call(body, terms, [HELD] * len(terms), [(out, HELD)], [], 10**6)[0]
        self.sent = sent
        came = around(after(sent, *wait) if wait else sent)
        if note:
            self.notes.append(came[rows:])
        self.came = came
        return came

    def finish(self):
        rows = self.rows
        came = self.came
        terms = [self.stay[4], self.came_from[4], came[rows : 2 * rows], sibling(came[:rows])]
        if self.far is not None:
            terms.append(self.far[4])
        return total(*terms)


def dot(a, b, dims):
    return lax.dot_general(a, b, (dims, ((), ())), preferred_element_type=F32)


NN, NT = ((1,), (0,)), ((1,), (1,))


def put_shards(order, pieces, target, sems):
    rows = pieces[0].shape[0]
    copies = []
    for n, piece in enumerate(pieces[:2]):
        to = pl.ds(pl.multiple_of(order[n], 16), rows)
        copies.append(load(piece, target.at[to, :], sems.at[n]))
    n = 2
    for piece in pieces[2:]:
        for part in range(piece.shape[0] // rows):
            to = pl.ds(pl.multiple_of(order[n], 16), rows)
            target[to, :] = piece[part * rows : (part + 1) * rows, :]
            n += 1
    wait_all(copies)


def load(source, target, sem):
    copy = pltpu.make_async_copy(source, target, sem)
    copy.start()
    return copy


def wait_all(copies):
    for copy in copies:
        copy.wait()


def allowed_bias(starts, bias):
    length = bias.shape[0]
    key_pos = lax.broadcasted_iota(jnp.int32, (length, 1), 0)
    query_pos = lax.broadcasted_iota(jnp.int32, (1, length), 1)
    key_series = jnp.zeros((length, 1), jnp.int32)
    query_series = jnp.zeros((1, length), jnp.int32)
    for n in range(starts.shape[1]):
        key_series += (starts[0, n] <= key_pos).astype(jnp.int32)
        query_series += (starts[0, n] <= query_pos).astype(jnp.int32)
    allowed = (key_pos <= query_pos) & (key_series == query_series)
    bias[...] = jnp.where(allowed, 0.0, -1e30).astype(F32)


def attend_kernel(heads, order, starts, scaling, normed, *rest):
    pieces, rest = rest[:10], rest[10:]
    keep, send, logsum, proj_out, weights_out, proj_t, weights, bias, scores, mixed, sems = rest
    cols = heads * HD
    length = normed.shape[0]
    allowed_bias(starts, bias)
    put_shards(order, pieces, weights, sems)
    stores = [load(weights, weights_out, sems.at[2])]
    for n in range(3):
        part = dot(normed[...], weights[:, n * cols : (n + 1) * cols], NN)
        if n == 0:
            part = part * scaling[...]
        proj_t[n * cols : (n + 1) * cols, :] = part.astype(BF16).T
    stores.append(load(proj_t, proj_out, sems.at[3]))
    blocks = ((0, length // 2), (length // 2, length))

    def rows(n, h):
        return pl.ds(pl.multiple_of(n * cols + h * HD, 16), HD)

    def one_head(h, slot):
        query = proj_t[rows(0, h), :]
        key = proj_t[rows(1, h), :].T
        value = proj_t[rows(2, h), :]
        for start, stop in blocks:
            scores[slot, :stop, start:stop] = dot(key[:stop], query[:, start:stop], NN)
        for start, stop in blocks:
            part = scores[slot, :stop, start:stop] + bias[:stop, start:stop]
            row_max = jnp.max(part, axis=0, keepdims=True)
            exponent = jnp.exp(part - row_max)
            total = jnp.sum(exponent, axis=0, keepdims=True)
            soft_b = (exponent * (1.0 / total)).astype(BF16)
            mixed[rows(0, h), start:stop] = dot(value[:, :stop], soft_b, NN).astype(BF16)
            logsum[h, :, start:stop] = row_max + jnp.log(total)

    @pl.loop(0, heads // UNROLL[0])
    def _(block):
        for n in range(UNROLL[0]):
            one_head(block * UNROLL[0] + n, n)

    half = order[16]
    low, high = mixed[:, : length // 2], mixed[:, length // 2 :]
    keep[...] = jnp.where(half == 0, low, high)
    send[...] = jnp.where(half == 0, high, low)
    wait_all(stores)


def assemble_kernel(order, *rest):
    here, there, (weights, sems) = rest[:10], rest[10:20], rest[20:]
    put_shards(order, here, weights.at[0], sems)
    put_shards(order, there, weights.at[1], sems)


def middle_kernel(
    tokens, cot, gain, keep, came, weights,
    dkeep, dsend, hidden_o, dup_o, normed_o, dattn_o, mixed_o, middle_o, dgain_o, dmiddle_out,
    dhidden, dmiddle_o, sem,
):
    cols = keep.shape[0]
    out, up, down = (slice(n * cols, (n + 1) * cols) for n in range(3))

    def half(n):
        return pl.ds(pl.multiple_of(n * cols, 128), cols)

    mixed_o[:, :cols] = keep[...].T
    mixed_o[:, cols:] = came[...].T
    middle_o[...] = tokens[...].astype(F32)

    @pl.loop(0, 2)
    def _(n):
        middle_o[...] += dot(mixed_o[:, half(n)], weights[n, :, out], NT)
        dhidden[:, half(n)] = dot(cot[...], weights[n, :, down], NN)

    middle = middle_o[...]
    scale = lax.rsqrt(jnp.mean(middle * middle, axis=-1, keepdims=True) + epsilon)
    normed_o[...] = (middle * scale * gain[...]).astype(BF16)

    @pl.loop(0, 2)
    def _(n):
        u = dot(normed_o[...], weights[n, :, up], NN)
        root = math.sqrt(2.0 / math.pi)
        square = u * u
        tanh = jnp.tanh(root * u * (1.0 + 0.044715 * square))
        gate = 0.5 * (1.0 + tanh)
        hidden_o[:, half(n)] = (u * gate).astype(BF16)
        slope = gate + 0.5 * u * (1.0 - tanh * tanh) * (root * (1.0 + 3 * 0.044715 * square))
        dup_o[:, half(n)] = (dhidden[:, half(n)] * slope).astype(BF16)

    dmiddle_o[...] = jnp.zeros_like(dmiddle_o)

    @pl.loop(0, 2)
    def _(n):
        dmiddle_o[...] += dot(dup_o[:, half(n)], weights[n, :, up], NT)

    dnormed = dmiddle_o[...]
    middle = middle_o[...]
    dgain_o[...] = jnp.sum(dnormed * middle * scale, axis=0, keepdims=True)
    weighted = dnormed * gain[...]
    mean = jnp.mean(weighted * middle, axis=-1, keepdims=True)
    dmiddle = cot[...].astype(F32) + scale * weighted - middle * (scale * scale * scale * mean)
    dmiddle_o[...] = dmiddle
    store = load(dmiddle_o, dmiddle_out, sem)
    dattn_o[...] = dmiddle.astype(BF16)
    for n, ref in enumerate((dkeep, dsend)):
        ref[...] = dot(dattn_o[...], weights[n, :, out], NN).astype(BF16).T
    store.wait()


def by_arrival(order, source_t, target, rows):
    for n, which in enumerate(LEAVE + STAY):
        target[n * rows : (n + 1) * rows, :] = source_t[
            pl.ds(pl.multiple_of(order[which], 16), rows), :
        ]


def split_rows(steps, rows, at=0):
    out = []
    for count in steps:
        out.append(slice(at, at + count * rows))
        at += count * rows
    return out


def late_grads_kernel(order, hidden, dup, normed, dattn, mixed, middle, weights, cot, *rest):
    outs, (grads, result, left_t, left, sems) = rest[:19], rest[19:]
    cols = dup.shape[1] // 2
    rows = dup.shape[1] // 16
    pairs = ((dattn, mixed), (normed, dup), (cot, hidden))
    for n, (a, _) in enumerate(pairs):
        left_t[n, :, :] = a[...].T
        by_arrival(order, left_t.at[n], left.at[n], rows)
    stores = []
    for leaves in range(2):
        top = leaves * 8 * rows
        part = slice(top, top + 8 * rows)
        for side, steps, start in ((1, FAR_STEPS, 10), (0, STEPS, 0)):
            for n, (_, b) in enumerate(pairs):
                grads[side, part, n * cols : (n + 1) * cols] = dot(
                    left[n, part, :], b[:, side * cols : (side + 1) * cols], NN
                ).astype(BF16)
            start += leaves * len(steps)
            for k, at in enumerate(split_rows(steps, rows, top)):
                stores.append(load(grads.at[side, at, :], outs[start + k], sems.at[start + k]))
    total = middle[...]
    for side in range(2):
        at = slice(side * cols, (side + 1) * cols)
        total = total + dot(hidden[:, at], weights[side, :, 2 * cols :], NT)
    result[...] = total.astype(BF16)
    stores.append(load(result, outs[18], sems.at[18]))
    wait_all(stores)


def attend_back_kernel(
    heads, order, starts, scaling_col, keep, came, logsum, proj_in, weights_in, tokens_in, other_in,
    dscaling, dgain, dproj_out, keep_out, send_out,
    weights, proj_t, bias, dmixed, dproj_t, scores, dsofts, dproj, kept, sent, tokens, sems,
):
    fetch = load(proj_in, proj_t, sems.at[0])
    fetch_late = [
        load(weights_in, weights, sems.at[1]),
        load(tokens_in, tokens.at[0], sems.at[2]),
        load(other_in, tokens.at[1], sems.at[3]),
    ]
    cols = heads * HD
    length = proj_t.shape[1]
    rows = length // 2
    allowed_bias(starts, bias)
    half = order[16]
    dmixed[:, :rows] = jnp.where(half == 0, keep[...], came[...])
    dmixed[:, rows:] = jnp.where(half == 0, came[...], keep[...])
    fetch.wait()
    dscaling[...] = jnp.zeros_like(dscaling)

    def place(n, h):
        return pl.ds(pl.multiple_of(n * cols + h * HD, 16), HD)

    def one_head(h, slot):
        query = proj_t[place(0, h), :]
        key_t = proj_t[place(1, h), :]
        key = key_t.T
        value = proj_t[place(2, h), :].T
        grad = dmixed[place(0, h), :]
        for start, stop in ((0, rows), (rows, length)):
            scores[slot, :stop, start:stop] = dot(key[:stop], query[:, start:stop], NN)
            dsofts[slot, :stop, start:stop] = dot(value[:stop], grad[:, start:stop], NN)
        parts = []
        for start, stop in ((rows, length), (0, rows)):
            soft = scores[slot, :stop, start:stop] + bias[:stop, start:stop]
            soft = jnp.exp(soft - logsum[h, :, start:stop])
            dsoft = dsofts[slot, :stop, start:stop]
            inner = jnp.sum(soft * dsoft, axis=0, keepdims=True)
            dscores = (soft * (dsoft - inner)).astype(BF16)
            dquery = dot(key_t[:, :stop], dscores, NN)
            dscaling[...] += jnp.sum(
                dquery * query[:, start:stop].astype(F32), axis=1, keepdims=True
            )
            dproj_t[place(0, h), start:stop] = (dquery * scaling_col[...]).astype(BF16)
            parts.append(
                (dot(dscores, query[:, start:stop], NT), dot(soft.astype(BF16), grad[:, start:stop], NT))
            )
        for n in range(2):
            both = jnp.concatenate([parts[0][n][:rows] + parts[1][n], parts[0][n][rows:]], axis=0)
            dproj_t[place(n + 1, h), :] = both.astype(BF16).T

    @pl.loop(0, heads // UNROLL[1])
    def _(block):
        for n in range(UNROLL[1]):
            one_head(block * UNROLL[1] + n, n % 2)

    dproj[...] = dproj_t[...].T
    stores = [load(dproj, dproj_out, sems.at[4])]
    wait_all(fetch_late)
    parts = []
    total = jnp.zeros(dgain.shape, F32)
    for n in range(2):
        part = dot(dproj[n * rows : (n + 1) * rows, :], weights[...], NT)
        resid = jnp.where(half == n, tokens[0], tokens[1]).astype(F32)
        scale = lax.rsqrt(jnp.mean(resid * resid, axis=-1, keepdims=True) + epsilon)
        total = total + jnp.sum(part * resid * scale, axis=0, keepdims=True)
        parts.append(part)
    dgain[...] = total
    sent[...] = jnp.where(half == 0, parts[1], parts[0]).astype(BF16)
    stores.append(load(sent, send_out, sems.at[5]))
    kept[...] = jnp.where(half == 0, parts[0], parts[1])
    stores.append(load(kept, keep_out, sems.at[6]))
    wait_all(stores)


def early_grads_kernel(order, normed, dproj_in, *rest):
    outs, (dproj, grads, left_t, left, sems) = rest[:10], rest[10:]
    fetch = load(dproj_in, dproj, sems.at[10])
    rows = normed.shape[1] // 16
    left_t[...] = normed[...].T
    by_arrival(order, left_t, left, rows)
    fetch.wait()
    stores = []
    for leaves in range(2):
        top = leaves * 8 * rows
        part = slice(top, top + 8 * rows)
        grads[part, :] = dot(left[part, :], dproj[...], NN).astype(BF16)
        for k, at in enumerate(split_rows(STEPS, rows, top)):
            n = 5 * leaves + k
            stores.append(load(grads.at[at, :], outs[n], sems.at[n]))
    wait_all(stores)


def first_kernel(stay, came, note, out):
    rows = stay.shape[0]
    out[:rows, :] = (stay[...].astype(F32) + came[...].astype(F32)).astype(BF16)
    out[rows:, :] = note[...]


def add_kernel(number, note, *rest):
    *terms, out = rest
    rows = terms[0].shape[0]
    late = terms.pop() if number > 0 else None
    part = terms[0][...].astype(F32)
    for term in terms[1:]:
        part = part + term[...].astype(F32)
    if number == 1:
        half = rows // 2
        out[:half, :] = part[:half].astype(BF16)
        out[half:rows, :] = (part[half:] + late[:half, :].astype(F32)).astype(BF16)
    else:
        if late is not None:
            part = part + late[:rows, :].astype(F32)
        out[:rows, :] = part.astype(BF16)
    if note:
        out[rows:, :] = late[late.shape[0] - 16 :, :]


def pair_kernel(one, other, out):
    out[...] = (one[...].astype(F32) + other[...].astype(F32)).astype(BF16)


def struct(*shape, kind=BF16):
    return jax.ShapeDtypeStruct(shape, kind)


def call(body, inputs, spaces, outputs, scratch, flops):
    place = {id(HELD): pltpu.VMEM, id(ANY): pltpu.HBM, id(VMEM): pltpu.HBM}
    inputs = [
        pltpu.with_memory_space_constraint(value, place[id(space)]) if id(space) in place else value
        for value, space in zip(inputs, spaces)
    ]
    return pl.pallas_call(
        body,
        out_shape=[place[id(space)](out.shape, out.dtype) for out, space in outputs],
        in_specs=[VMEM if space is HELD else space for space in spaces],
        out_specs=[VMEM if space is HELD else space for _, space in outputs],
        scratch_shapes=scratch,
        compiler_params=pltpu.CompilerParams(vmem_limit_bytes=LIMIT),
        cost_estimate=pl.CostEstimate(flops=flops * 4, bytes_accessed=2**22, transcendentals=0),
    )(*inputs)


def in_order(half, own, other, axis=0):
    return jnp.where(
        half == 0,
        jnp.concatenate([own, other], axis=axis),
        jnp.concatenate([other, own], axis=axis),
    )


def on_slice(
    tokens,
    seg_starts,
    gain_attn,
    gain_mlp,
    query_scale,
    w_query,
    w_key,
    w_value,
    w_out,
    w_up,
    w_down,
    cotangent,
):
    half = lax.axis_index("tp")
    rows, width = tokens.shape
    shard, cols = w_query.shape
    length = 2 * rows
    heads = cols // HD
    dma = pltpu.SemaphoreType.DMA
    order = arrival_order(shard)
    early, late = call(
        pack_kernel,
        [w_query, w_key, w_value, w_out.T, w_up, w_down.T],
        [VMEM] * 6,
        [(struct(shard, 3 * cols), VMEM)] * 2,
        [],
        10**6,
    )

    def prepare(other_tokens):
        row_tokens = in_order(half, tokens, other_tokens).astype(F32)
        return (row_tokens * inverse_rms(row_tokens) * gain_attn).astype(BF16)

    first, here, there, normed, other_tokens = ring_gather(early, late, tokens, prepare)
    scaling = softplus_unit / math.sqrt(HD) * jax.nn.softplus(query_scale)
    keep, send, logsum, proj_t, w_in = call(
        functools.partial(attend_kernel, heads),
        [after(order, there[2]), seg_starts, jnp.tile(scaling, heads)[None, :], normed]
        + first,
        [SMEM] * 2 + [HELD] * 2 + [ANY] * 2 + [HELD] * 8,
        [
            (struct(cols, rows), HELD),
            (struct(cols, rows), HELD),
            (struct(heads, 1, length, kind=F32), HELD),
            (struct(3 * cols, length), ANY),
            (struct(width, 3 * cols), ANY),
        ],
        [
            pltpu.VMEM((3 * cols, length), BF16),
            pltpu.VMEM((width, 3 * cols), BF16),
            pltpu.VMEM((length, length), F32),
            pltpu.VMEM((UNROLL[0], length, length), F32),
            pltpu.VMEM((cols, length), BF16),
            dma((4,)),
        ],
        8 * 10**9,
    )
    came = across(send)
    here, there = swap_late(here, there, logsum)
    w_late = call(
        assemble_kernel,
        [order, *here, *there],
        [SMEM] + ([ANY] * 2 + [HELD] * 8) * 2,
        [(struct(2, width, 3 * cols), HELD)],
        [dma((2,))],
        10**6,
    )[0]
    act = struct(rows, width)
    dkeep, dsend, *saved, dgain_two, dmiddle = call(
        middle_kernel,
        [tokens, cotangent, gain_mlp[None, :], keep, came, w_late],
        [HELD] * 6,
        [(struct(cols, rows), HELD)] * 2
        + [(act, HELD)] * 5
        + [
            (struct(rows, width, kind=F32), HELD),
            (struct(1, width, kind=F32), HELD),
            (struct(rows, width, kind=F32), ANY),
        ],
        [pltpu.VMEM((rows, width), F32), pltpu.VMEM((rows, width), F32), dma],
        8 * 10**9,
    )
    dcame = across(dsend)
    *parts, result = call(
        late_grads_kernel,
        [order, *saved, w_late, cotangent],
        [SMEM] + [HELD] * 8,
        [(struct(n * shard, 3 * cols), ANY) for n in STEPS * 2 + FAR_STEPS * 2] + [(act, ANY)],
        [
            pltpu.VMEM((2, width, 3 * cols), BF16),
            pltpu.VMEM((rows, width), BF16),
            pltpu.VMEM((3, width, rows), BF16),
            pltpu.VMEM((3, width, rows), BF16),
            dma((19,)),
        ],
        6 * 10**9,
    )
    *parts, result = all_after((*parts, result), dcame)
    far, far_sent = [], []
    for n, steps in enumerate(FAR_STEPS):
        pair = [parts[14 + n], sibling(parts[10 + n])]
        sent = call(pair_kernel, pair, [HELD] * 2, [(struct(steps * shard, 3 * cols), HELD)], [], 10**6)
        far_sent += sent
        far.append(across(sent[0]))
    far_last = far.pop()
    far += [far_last[: 2 * shard], far_last[2 * shard :]]
    late_sum = Scatter(parts[:10], far)
    late_one = late_sum.step(0)
    dscaling, dgain_one, dproj, dnormed, dnormed_send = call(
        functools.partial(attend_back_kernel, heads),
        [
            after(order, late_sum.came_from[0]),
            seg_starts,
            scaling[:, None],
            dkeep,
            dcame,
            logsum,
            proj_t,
            w_in,
            tokens,
            other_tokens,
        ],
        [SMEM] * 2 + [HELD] * 4 + [ANY] * 4,
        [
            (struct(HD, 1, kind=F32), HELD),
            (struct(1, width, kind=F32), HELD),
            (struct(length, 3 * cols), ANY),
            (struct(rows, width, kind=F32), ANY),
            (act, ANY),
        ],
        [
            pltpu.VMEM((width, 3 * cols), BF16),
            pltpu.VMEM((3 * cols, length), BF16),
            pltpu.VMEM((length, length), F32),
            pltpu.VMEM((cols, length), BF16),
            pltpu.VMEM((3 * cols, length), BF16),
            pltpu.VMEM((2, length, length), F32),
            pltpu.VMEM((2, length, length), F32),
            pltpu.VMEM((length, 3 * cols), BF16),
            pltpu.VMEM((rows, width), F32),
            pltpu.VMEM((rows, width), BF16),
            pltpu.VMEM((2, rows, width), BF16),
            dma((7,)),
        ],
        12 * 10**9,
    )
    dscaling, dgain_one, dproj, dnormed, dnormed_send = all_after(
        (dscaling, dgain_one, dproj, dnormed, dnormed_send), *far[:2]
    )
    dscale_param = (
        dscaling[:, 0] / scaling * (softplus_unit / math.sqrt(HD)) * jax.nn.sigmoid(query_scale)
    )
    note = jnp.concatenate(
        [
            jnp.concatenate([dgain_one, jnp.pad(dscale_param[None, :], ((0, 0), (0, cols - HD)))], axis=1),
            jnp.pad(dgain_two, ((0, 0), (0, cols))),
        ]
    )
    parts = call(
        early_grads_kernel,
        [after(order, far_sent[2]), normed, dproj],
        [SMEM, HELD, ANY],
        [(struct(n * shard, 3 * cols), ANY) for n in STEPS + STEPS],
        [
            pltpu.VMEM((length, 3 * cols), BF16),
            pltpu.VMEM((width, 3 * cols), BF16),
            pltpu.VMEM((width, length), BF16),
            pltpu.VMEM((width, length), BF16),
            dma((11,)),
        ],
        5 * 10**9,
    )
    note = note + sibling(after(note, parts[1]))
    high = lax.reduce_precision(note, 8, 7)
    coded = jnp.concatenate([high, note - high, jnp.zeros((12, 3 * cols), F32)]).astype(BF16)
    parts = all_after(parts, late_one)
    late_two = late_sum.step(1)
    early_sum = Scatter(parts, note=coded)
    early_sum.step(0)
    late_three = late_sum.step(2)
    early_sum.came = after(early_sum.came, late_two)
    early_sum.step(1)
    late_four = late_sum.step(3)
    early_three = early_sum.step(2)
    dnormed = dnormed + after(across(dnormed_send), early_three).astype(F32)
    resid = tokens.astype(F32)
    dresid_one, _ = norm_backward(resid, inverse_rms(resid), gain_attn, dnormed)
    early_sum.came = after(early_sum.came, late_three, far[3])
    early_sum.step(3)
    late_sum.came = after(late_sum.came, early_sum.sent)
    dlate = late_sum.finish()
    din = early_sum.finish()
    mine = early_sum.notes
    core = lax.rem(lax.axis_index("fsdp"), 2)
    heard = total(*mine[:3]) + jnp.where(core == 0, 1.0, 0.0) * mine[3].astype(F32)
    heard = heard[:2] + heard[2:4]
    heard = heard + sibling(heard)
    small = note + heard
    small = small + across(small)
    return (
        result,
        dmiddle + dresid_one,
        small[0, :width],
        small[1, :width],
        small[0, width : width + HD],
        din[:, :cols],
        din[:, cols : 2 * cols],
        din[:, 2 * cols :],
        dlate[:, :cols].T,
        dlate[:, cols : 2 * cols],
        dlate[:, 2 * cols :].T,
    )


def solution(mesh):
    body = on_slice if dict(mesh.shape) == {"fsdp": 16, "tp": 2} else on_device
    placed = (
        P(("fsdp", "tp"), None),
        P("fsdp", None),
        P(),
        P(),
        P(),
        P("fsdp", "tp"),
        P("fsdp", "tp"),
        P("fsdp", "tp"),
        P("tp", "fsdp"),
        P("fsdp", "tp"),
        P("tp", "fsdp"),
        P(("fsdp", "tp"), None),
    )
    return jax.shard_map(
        body,
        mesh=mesh,
        in_specs=placed,
        out_specs=(
            P(("fsdp", "tp"), None),
            P(("fsdp", "tp"), None),
            P(),
            P(),
            P(),
            P("fsdp", "tp"),
            P("fsdp", "tp"),
            P("fsdp", "tp"),
            P("tp", "fsdp"),
            P("fsdp", "tp"),
            P("tp", "fsdp"),
        ),
        check_vma=False,
    )
```
